32 devices in a mesh: row: 4 (over z), col: 8 (over y, x, core).
Axes of the slice: x: 2, y: 2, z: 4, core: 2. Of those that a mesh axis runs over, the one named last changes fastest.
Arguments:
- tiles: bfloat16 [4, 8, 16, 576, 576], P('row', 'col'), may hold values from -0.0625 to 0.0625
- diag_tiles: bfloat16 [32, 576, 576], P(('row', 'col')), as said below
- probes: float32 [32, 64, 576], P(('row', 'col'))
- rows_list: int32 [4, 8, 16], P('row', 'col'), may hold values from 0 to 7, as said below
- cols_list: int32 [4, 8, 16], P('row', 'col'), may hold values from 0 to 3, as said below
- counts: int32 [4, 8], P('row', 'col'), may hold values from 0 to 16, as said below
Outputs:
- solution: float32 [32, 64, 576], P(('row', 'col'))
- residual: float32 [32, 64, 576], P(('row', 'col'))
The draws below stay inside these ranges and needn't reach their ends.
Inputs may be any that keep to these rules, and one draw needn't show every extreme that they name: `rows_list`: slots past a device's count hold 0; a held slot lies strictly below the diagonal. `cols_list`: slots past a device's count hold 0. `counts`: the busiest device holds 16 tiles. `diag_tiles`: each diagonal tile is symmetric positive definite: its diagonal entries are at least 4.4 and its off-diagonal part has spectral radius below about 1.
All inputs are finite; a program needn't handle non-finite values.
Results may differ from the reference program's by a relative error of at most 0.039.
Values may be sent and summed in bfloat16 or wider, within the bound.
No kernel may reach another device: no remote copies, remote signals or barrier semaphores. Data moves between devices by JAX's collectives and lax.ppermute only.
A program may use at most 128 MiB of HBM per device.

```python
import math
import jax
import jax.numpy as jnp
from jax import lax

B = 576
P_SIZE = 64
KMAX = 16
ITERS = 2
ROW_BLOCKS = 4
COL_BLOCKS = 8
NT = 32


def tile_lists(key):
    keys = jax.random.split(jax.random.fold_in(key, 7), 3)
    shape = (ROW_BLOCKS, COL_BLOCKS, KMAX)
    rows = jnp.arange(ROW_BLOCKS)[:, None, None]
    cols = jnp.arange(COL_BLOCKS)[None, :, None]
    slots = jnp.arange(KMAX)[None, None, :]
    first = jax.random.randint(keys[0], shape, 0, 1 << 20)
    second = jax.random.randint(keys[1], shape, 0, 1 << 20)
    third = jax.random.randint(keys[2], (ROW_BLOCKS, COL_BLOCKS), 0, 1 << 20)
    lastcol = cols == COL_BLOCKS - 1
    source = first % (rows + 1)
    source = jnp.where((source == rows) & lastcol, rows - 1, source)
    forced = (rows == ROW_BLOCKS - 1) & (cols == 0) & (slots == 0)
    source = jnp.where(forced, ROW_BLOCKS - 1, source)
    room = jnp.maximum(COL_BLOCKS - 1 - cols, 1)
    local = jnp.where(source == rows, cols + 1 + second % room, second % COL_BLOCKS)
    rr = jnp.arange(ROW_BLOCKS)[:, None]
    cc = jnp.arange(COL_BLOCKS)[None, :]
    count = jnp.maximum(1, KMAX * (rr + 1) // ROW_BLOCKS - third % 2)
    count = jnp.where((rr == ROW_BLOCKS - 1) & (cc == 0), KMAX, count)
    count = jnp.where((rr == 0) & (cc == COL_BLOCKS - 1), 0, count)
    held = slots < count[:, :, None]
    local = jnp.where(held, local, 0)
    source = jnp.where(held, source, 0)
    return (local.astype(jnp.int32), source.astype(jnp.int32), count.astype(jnp.int32))


def draw_rows_list(key, part):
    return tile_lists(key)[0]


def draw_cols_list(key, part):
    return tile_lists(key)[1]


def draw_counts(key, part):
    return tile_lists(key)[2]


def draw_diag_tiles(key, part):
    keys = jax.random.split(jax.random.fold_in(key, 11), 2)
    noise = jax.random.normal(keys[0], (NT, B, B), jnp.float32) * (0.5 / math.sqrt(B))
    lift = jax.random.uniform(keys[1], (NT, B), jnp.float32, 5.0, 7.0)
    sym = 0.5 * (noise + jnp.swapaxes(noise, 1, 2))
    full = sym + jnp.eye(B, dtype=jnp.float32)[None, :, :] * lift[:, None, :]
    return full.astype(jnp.bfloat16)


def draw_probes(key, part):
    keys = jax.random.split(jax.random.fold_in(key, 13), 1)
    ramp = 1.0 + 2.0 * jnp.arange(NT, dtype=jnp.float32) / (NT - 1)
    values = jax.random.normal(keys[0], (NT, P_SIZE, B), jnp.float32)
    return values * ramp[:, None, None]


def shard_levels(key, dims, cuts, smallest, high):
    level, own = 1.0, jax.random.fold_in(key, 6)
    for axis_at, blocks in cuts:
        draws = jnp.exp(jax.random.uniform(jax.random.fold_in(own, axis_at), (blocks,), jnp.float32, smallest / len(cuts), high / len(cuts)))
        level = level * jnp.repeat(draws, dims[axis_at] // blocks).reshape([-1 if axis == axis_at else 1 for axis in range(len(dims))])
    return level


def centred(key, extent, width, limit, shards=(), kind=jnp.bfloat16):
    result = jax.random.normal(key, extent, jnp.float32) * width
    if len(shards) > 0:
        result = shard_levels(key, extent, shards, -0.22, 0.18) * result
    return jnp.clip(result, min=-limit, max=limit).astype(kind)


def setup_inputs(seed: int = 0) -> dict:
    key_of = jax.random.split(jax.random.key(seed), 7)
    tiles = centred(key_of[0], (ROW_BLOCKS, COL_BLOCKS, KMAX, B, B), (16 * B) ** -0.5, 0.0625, ((0, 4), (1, 8)))
    diag_tiles = draw_diag_tiles(jax.random.fold_in(key_of[6], 71), 0)
    probes = draw_probes(jax.random.fold_in(key_of[6], 71), 0)
    rows_list = draw_rows_list(jax.random.fold_in(key_of[6], 71), 0)
    cols_list = draw_cols_list(jax.random.fold_in(key_of[6], 71), 0)
    counts = draw_counts(jax.random.fold_in(key_of[6], 71), 0)
    return {"tiles": tiles, "diag_tiles": diag_tiles, "probes": probes, "rows_list": rows_list, "cols_list": cols_list, "counts": counts}


def gram(left, right):
    return jnp.einsum('tpb,tqb->pq', left, right, precision=lax.Precision.HIGHEST)

def combine(coef, block):
    return jnp.einsum('pq,tpb->tqb', coef, block, precision=lax.Precision.HIGHEST)

def solve_with(matrix, rhs):
    factor = jnp.linalg.cholesky(matrix)
    middle = lax.linalg.triangular_solve(factor, rhs, left_side=True, lower=True, transpose_a=False)
    return lax.linalg.triangular_solve(factor, middle, left_side=True, lower=True, transpose_a=True)

def operator(tiles, diag_tiles, rows_list, cols_list, counts, direction):
    rounded = direction.astype(jnp.bfloat16)
    slots = jnp.arange(KMAX)

    def visit(acc, dev):
        r = dev // COL_BLOCKS
        c = dev % COL_BLOCKS
        blocks = tiles[r, c].astype(jnp.float32)
        valid = (slots < counts[r, c]).astype(jnp.float32)[:, None, None]
        grow = (r * COL_BLOCKS + rows_list[r, c]).astype(jnp.int32)
        gcol = (cols_list[r, c] * COL_BLOCKS + c).astype(jnp.int32)
        near = rounded[grow].astype(jnp.float32)
        far = rounded[gcol].astype(jnp.float32)
        fwd = jnp.einsum('kpb,kcb->kpc', far, blocks) * valid
        bwd = jnp.einsum('kpb,kbc->kpc', near, blocks) * valid
        acc = acc.at[grow].add(fwd)
        acc = acc.at[gcol].add(bwd)
        own = lax.dot_general(rounded[dev].astype(jnp.float32), diag_tiles[dev].astype(jnp.float32), (((1,), (1,)), ((), ())), preferred_element_type=jnp.float32)
        acc = acc.at[dev].add(own)
        return (acc, None)
    start = jnp.zeros(direction.shape, jnp.float32)
    image, unused = lax.scan(visit, start, jnp.arange(NT).astype(jnp.int32))
    return image

def reference(tiles, diag_tiles, probes, rows_list, cols_list, counts):
    solution = jnp.zeros(probes.shape, jnp.float32)
    residual = probes
    direction = probes
    norm_now = gram(residual, residual)
    for step in range(ITERS):
        image = operator(tiles, diag_tiles, rows_list, cols_list, counts, direction)
        curv = gram(direction, image)
        alpha = solve_with(curv, norm_now)
        solution = solution + combine(alpha, direction)
        residual = residual - combine(alpha, image)
        if step + 1 < ITERS:
            norm_next = gram(residual, residual)
            beta = solve_with(norm_now, norm_next)
            direction = residual + combine(beta, direction)
            norm_now = norm_next
    return (solution, residual)
```

```python
import functools

import jax
import jax.numpy as jnp
from jax import lax
from jax.experimental import pallas as pl
from jax.experimental.pallas import tpu as pltpu
from jax.sharding import PartitionSpec as P

ITERS = 2
F32 = jnp.float32
BF16 = jnp.bfloat16
HI = lax.Precision.HIGHEST
NT = (((1,), (1,)), ((), ()))
NN = (((1,), (0,)), ((), ()))
TN = (((0,), (0,)), ((), ()))
VMEM = pl.BlockSpec(memory_space=pltpu.VMEM)
SMEM = pl.BlockSpec(memory_space=pltpu.SMEM)
ANY = pl.BlockSpec(memory_space=pl.ANY)


def dot32(left, right, dims):
    return lax.dot_general(left, right, dims, precision=HI, preferred_element_type=F32)


def dot16(left, right, dims):
    return lax.dot_general(left, right, dims, preferred_element_type=F32)


def dot_exact16(left, right, dims):
    first = right.astype(BF16)
    rest = right - first.astype(F32)
    second = rest.astype(BF16)
    third = (rest - second.astype(F32)).astype(BF16)
    return dot16(left, first, dims) + (dot16(left, second, dims) + dot16(left, third, dims))


def eliminate(systems):
    size = systems[0].shape[0]
    rows = lax.broadcasted_iota(jnp.int32, (size, 1), 0)
    for k in range(size):
        after = []
        for system in systems:
            row = system[k : k + 1, :]
            pivot = row[:, k : k + 1]
            scaled = row * (1.0 / pivot)
            after.append(jnp.where(rows == k, scaled, system - system[:, k : k + 1] * scaled))
        systems = after
    return [system[:, size:] for system in systems]


def operator_kernel(
    counts, rows_at, cols_at, near_own, near_far, *rest, n_row, n_chip, slots
):
    far_in = rest[:n_row]
    tiles, diag, extra = rest[n_row : n_row + 3]
    out = rest[n_row + 3 :]
    give_core, keep = out[0], out[1]
    give_row = out[2 : 2 + n_row - 1]
    grams = out[2 + n_row - 1]
    near, far, acc_row, acc_col, held, arrived = out[2 + n_row :]
    count = counts[0]

    def fetch(slot):
        return pltpu.make_async_copy(tiles.at[slot], held.at[slot], arrived.at[slot])

    def begin(slot, carry):
        fetch(slot).start()
        return carry

    lax.fori_loop(0, count, begin, 0)
    for d in range(n_chip):
        near[d] = near_own[d]
        near[n_chip + d] = near_far[d]
    for d in range(n_row):
        far[d] = far_in[d][...]
    acc_row[...] = jnp.zeros_like(acc_row)
    acc_col[...] = jnp.zeros_like(acc_col)
    mine = near_own[0]
    own = dot16(mine, diag[...], NT)
    p_size = own.shape[0]

    def turn(slot, carry):
        fetch(slot).wait()
        tile = held[slot]
        i = rows_at[slot]
        j = cols_at[slot]
        acc_row[i] += dot16(far[j], tile, NT)
        acc_col[j] += dot16(near[i], tile, NN)
        return carry

    lax.fori_loop(0, count, turn, 0)
    half = dot_exact16(far[0], acc_col[0], NT)
    for d in range(1, n_row):
        half += dot_exact16(far[d], acc_col[d], NT)
        give_row[d - 1][...] = acc_col[d].astype(BF16)
    grams[:, :p_size] = half + half.T + dot_exact16(mine, own, NT)
    grams[:, p_size:] = extra[...]
    for d in range(n_chip):
        give_core[d] = acc_row[n_chip + d].astype(BF16)
        keep[d] = acc_row[d]
    keep[0] += own + acc_col[0]


def join_kernel(keep, came, grams, grams_came, mine, *give):
    mine[...] = keep[0] + came[0].astype(F32)
    for d in range(1, keep.shape[0]):
        give[d - 1][...] = (keep[d] + came[d].astype(F32)).astype(BF16)
    give[-1][...] = grams[...] + grams_came[...]


def sum_kernel(*refs):
    total = refs[0][...]
    for ref in refs[1:-1]:
        total += ref[...]
    refs[-1][...] = total


def first_kernel(mine, probes, *rest, n_in, n_gram):
    image = mine[...]
    for ref in rest[:n_in]:
        image += ref[...].astype(F32)
    total = rest[n_in][...]
    for ref in rest[n_in + 1 : n_in + n_gram]:
        total += ref[...]
    image_out, residual_out, rounded, extra, small = rest[n_in + n_gram :]
    size = image.shape[0]
    curv = total[:, :size]
    norm = total[:, size : 2 * size]
    eye = (
        lax.broadcasted_iota(jnp.int32, (size, size), 0)
        == lax.broadcasted_iota(jnp.int32, (size, size), 1)
    ).astype(F32)
    alpha, inverse = eliminate(
        [jnp.concatenate([curv, norm], 1), jnp.concatenate([norm, eye], 1)]
    )
    residual = probes[...] - dot32(alpha, image, TN)
    image_out[...] = image
    residual_out[...] = residual
    rounded[...] = residual.astype(BF16)
    extra[:, :size] = dot32(residual, residual, NT)
    extra[:, size:] = dot32(image, residual, NT)
    small[0] = curv
    small[1] = alpha
    small[2] = inverse


def last_kernel(mine, probes, image_in, residual_in, small, *rest, n_in, n_gram):
    forward = mine[...]
    for ref in rest[:n_in]:
        forward += ref[...].astype(F32)
    total = rest[n_in][...]
    for ref in rest[n_in + 1 : n_in + n_gram]:
        total += ref[...]
    solution_out, residual_out = rest[n_in + n_gram :]
    size = forward.shape[0]
    curv, alpha, inverse = small[0], small[1], small[2]
    norm = total[:, size : 2 * size]
    cross = total[:, 2 * size :]
    beta = dot32(inverse, norm, NN)
    mixed = dot32(cross, beta, TN)
    curv_next = total[:, :size] + mixed + mixed.T + dot32(beta, dot32(curv, beta, NN), TN)
    (step,) = eliminate([jnp.concatenate([curv_next, norm], 1)])
    both = dot32(beta, step, NN)
    residual = residual_in[...]
    solution_out[...] = dot32(alpha + both, probes[...], TN) + dot32(step, residual, TN)
    residual_out[...] = residual - dot32(step, forward, TN) - dot32(both, image_in[...], TN)


def call(kernel, outs, args, specs=None, scratch=(), limit=48, name=None):
    return pl.pallas_call(
        kernel,
        out_shape=outs,
        in_specs=[VMEM] * len(args) if specs is None else specs,
        out_specs=[VMEM] * len(outs),
        scratch_shapes=list(scratch),
        compiler_params=pltpu.CompilerParams(vmem_limit_bytes=limit << 20),
        name=name,
    )(*args)


def body(n_row, n_col, tiles, diag_tiles, probes, rows_list, cols_list, counts):
    n_chip = n_col // 2
    p_size, width = probes.shape[1:]
    slots = tiles.shape[2]
    shape = jax.ShapeDtypeStruct
    block32 = shape((p_size, width), F32)
    block16 = shape((p_size, width), BF16)

    def over(value, axis, delta):
        size = n_row if axis == "row" else n_col
        return lax.ppermute(value, axis, [(i, i ^ delta) for i in range(size)])

    def over_chips(value):
        return [over(value, "col", 2 * d) for d in range(1, n_chip)]

    def over_rows(value):
        return [over(value, "row", d) for d in range(1, n_row)]

    apart = rows_list[0, 0] ^ lax.axis_index("col")
    rows_at = (apart % 2) * n_chip + apart // 2
    cols_at = cols_list[0, 0] ^ lax.axis_index("row")
    probes = probes[0]

    def apply_operator(rounded, extra):
        far = [rounded] + over_rows(rounded)
        near_own = jnp.stack([rounded] + over_chips(rounded))
        near_far = over(near_own, "col", 1)
        args = [counts[0], rows_at, cols_at, near_own, near_far, *far, tiles[0, 0], diag_tiles[0], extra]
        specs = [SMEM] * 3 + [VMEM] * (2 + n_row) + [ANY, VMEM, VMEM]
        outs = [shape((n_chip, p_size, width), BF16), shape((n_chip, p_size, width), F32)]
        outs += [block16] * (n_row - 1) + [shape((p_size, 3 * p_size), F32)]
        scratch = [
            pltpu.VMEM((n_col, p_size, width), BF16),
            pltpu.VMEM((n_row, p_size, width), BF16),
            pltpu.VMEM((n_col, p_size, width), F32),
            pltpu.VMEM((n_row, p_size, width), F32),
            pltpu.VMEM((slots, width, width), BF16),
            pltpu.SemaphoreType.DMA((slots,)),
        ]
        kernel = functools.partial(operator_kernel, n_row=n_row, n_chip=n_chip, slots=slots)
        got = call(kernel, outs, args, specs, scratch, name="operator")
        give_core, keep, give_row, grams = got[0], got[1], got[2:-1], got[-1]
        came = over(give_core, "col", 1)
        grams_came = over(grams, "col", 1)
        from_rows = [over(block, "row", d + 1) for d, block in enumerate(give_row)]
        outs = [block32] + [block16] * (n_chip - 1) + [shape(grams.shape, F32)]
        got = call(join_kernel, outs, [keep, came, grams, grams_came], name="join")
        from_chips = [over(block, "col", 2 * d + 2) for d, block in enumerate(got[1:-1])]
        grams = got[-1]
        chip_grams = [grams] + over_chips(grams)
        (grams,) = call(sum_kernel, [shape(grams.shape, F32)], chip_grams, name="gram_sum")
        return got[0], from_chips + from_rows, [grams] + over_rows(grams)

    norm = dot32(probes, probes, NT)
    extra = jnp.concatenate([norm, jnp.zeros_like(norm)], 1)
    mine, parts, grams = apply_operator(probes.astype(BF16), extra)
    outs = [block32, block32, block16, shape((p_size, 2 * p_size), F32), shape((3, p_size, p_size), F32)]
    counted = {"n_in": len(parts), "n_gram": len(grams)}
    image, residual, rounded, extra, small = call(
        functools.partial(first_kernel, **counted), outs, [mine, probes, *parts, *grams], name="first_step"
    )
    mine, parts, grams = apply_operator(rounded, extra)
    solved, residual = call(
        functools.partial(last_kernel, **counted),
        [block32, block32],
        [mine, probes, image, residual, small, *parts, *grams],
        name="last_step",
    )
    return solved[None], residual[None]


def solution(mesh):
    placed = (
        P("row", "col", None, None, None),
        P(("row", "col"), None, None),
        P(("row", "col"), None, None),
        P("row", "col", None),
        P("row", "col", None),
        P("row", "col"),
    )
    return jax.shard_map(
        functools.partial(body, mesh.shape["row"], mesh.shape["col"]),
        mesh=mesh,
        in_specs=placed,
        out_specs=(P(("row", "col"), None, None), P(("row", "col"), None, None)),
        check_vma=False,
    )
```

```python
import functools

import jax
import jax.numpy as jnp
from jax import lax
from jax.experimental import pallas as pl
from jax.experimental.pallas import tpu as pltpu
from jax.sharding import PartitionSpec as P

ITERS = 2
F32 = jnp.float32
BF16 = jnp.bfloat16
HI = lax.Precision.HIGHEST
NT = (((1,), (1,)), ((), ()))
NN = (((1,), (0,)), ((), ()))
TN = (((0,), (0,)), ((), ()))
ANY = pl.BlockSpec(memory_space=pl.ANY)
VMEM = pl.BlockSpec(memory_space=pltpu.VMEM)
SMEM = pl.BlockSpec(memory_space=pltpu.SMEM)


def dot32(left, right, dims):
    return lax.dot_general(left, right, dims, precision=HI, preferred_element_type=F32)


def dot16(left, right, dims):
    return lax.dot_general(left, right, dims, preferred_element_type=F32)


def dot_exact16(left, right, dims):
    first = right.astype(BF16)
    rest = right - first.astype(F32)
    second = rest.astype(BF16)
    third = (rest - second.astype(F32)).astype(BF16)
    return dot16(left, first, dims) + (dot16(left, second, dims) + dot16(left, third, dims))


def eliminate(systems, group=8):
    size, width = systems[0].shape
    rows = lax.broadcasted_iota(jnp.int32, (size, width), 0)
    for start in range(0, size, group):
        after = []
        for system in systems:
            columns = [
                jnp.broadcast_to(system[:, k : k + 1], (size, width)) for k in range(start, start + group)
            ]
            for place, k in enumerate(range(start, start + group)):
                inverse = 1.0 / columns[place][k : k + 1, :]
                here = rows == k
                scaled = system[k : k + 1, :] * inverse
                for later in range(place + 1, group):
                    factor = columns[later][k : k + 1, :] * inverse
                    columns[later] = jnp.where(here, factor, columns[later] - columns[place] * factor)
                system = jnp.where(here, scaled, system - columns[place] * scaled)
            after.append(system)
        systems = after
    return [system[:, size:] for system in systems]


def split16(value):
    first = value.astype(BF16)
    return first, (value - first.astype(F32)).astype(BF16)


def pack(block, grams):
    size = grams.shape[0]
    rows = lax.broadcasted_iota(jnp.int32, (size, size), 0)
    columns = lax.broadcasted_iota(jnp.int32, (size, size), 1)
    both = jnp.where(rows >= columns, grams[:, :size], grams[:, size:])
    diagonal = jnp.sum(jnp.where(rows == columns, grams[:, size:], 0.0), axis=1, keepdims=True)
    first, second = split16(both)
    top, rest = split16(jnp.broadcast_to(diagonal, (size, size)))
    return jnp.concatenate([block, first, second, jnp.where(columns == 0, top, rest)], 1)


def unpack(message, width):
    size = message.shape[0]
    parts = message[:, width:].astype(F32)
    both = parts[:, :size] + parts[:, size : 2 * size]
    diagonal = parts[:, 2 * size : 2 * size + 1] + parts[:, 2 * size + 1 : 2 * size + 2]
    rows = lax.broadcasted_iota(jnp.int32, (size, size), 0)
    columns = lax.broadcasted_iota(jnp.int32, (size, size), 1)
    turned = both.T
    first = jnp.where(rows >= columns, both, turned)
    second = jnp.where(rows < columns, both, turned)
    return jnp.concatenate([first, jnp.where(rows == columns, diagonal, second)], 1)


def held_slots(count, slots, work):
    group = 4 if slots % 4 == 0 else 1

    def turn(g, carry):
        for u in range(group):
            slot = g * group + u
            work(slot, slot < count)
        return carry

    lax.fori_loop(0, (count + group - 1) // group, turn, 0)


def load_kernel(index, tiles, out, arrived):
    def fetch(slot):
        return pltpu.make_async_copy(tiles.at[slot], out.at[slot], arrived.at[slot])

    def begin(slot, carry):
        fetch(slot).start()
        return carry

    def end(slot, carry):
        fetch(slot).wait()
        return carry

    lax.fori_loop(0, index[0], begin, 0)
    lax.fori_loop(0, index[0], end, 0)


def mirrored_kernel(index, near_own, near_far, tiles, diag, acc, own, near):
    n_chip = near_own.shape[0]
    slots = tiles.shape[0]
    for d in range(n_chip):
        near[d] = near_own[d]
        near[n_chip + d] = near_far[d]
    acc[...] = jnp.zeros_like(acc)

    def work(slot, held):
        i = index[1 + slot]
        j = index[1 + slots + slot]
        acc[j] += jnp.where(held, dot16(near[i], tiles[slot], NN), 0.0)

    held_slots(index[0], slots, work)
    own[...] = dot16(near_own[0], diag[...], NT)


def gram_kernel(acc, own, residual, *rest):
    n_row, size = acc.shape[0], own.shape[0]
    far, grams, give = rest[:n_row], rest[n_row], rest[n_row + 1 :]
    half = dot_exact16(far[0][...], acc[0] + 0.5 * own[...], NT)
    for d in range(1, n_row):
        half += dot_exact16(far[d][...], acc[d], NT)
    total = jnp.concatenate([half + half.T, dot32(residual[...], residual[...], NT)], 1)
    grams[...] = total
    for d in range(1, n_row):
        give[d - 1][...] = pack(acc[d].astype(BF16), total)


def forward_kernel(index, tiles, after, *rest, n_row):
    far_in = rest[:n_row]
    give_core, keep, far, acc = rest[n_row:]
    n_chip = keep.shape[0]
    slots = tiles.shape[0]
    for d in range(n_row):
        far[d] = far_in[d][...]
    acc[...] = jnp.zeros_like(acc)

    def work(slot, held):
        i = index[1 + slot]
        j = index[1 + slots + slot]
        acc[i] += jnp.where(held, dot16(far[j], tiles[slot], NT), 0.0)

    held_slots(index[0], slots, work)
    for d in range(n_chip):
        give_core[d] = acc[n_chip + d].astype(BF16)
        keep[d] = acc[d]


def rows_kernel(grams, *rest):
    *came, out = rest
    total = grams[...]
    for message in came:
        total += unpack(message[...], message.shape[1] - 3 * grams.shape[0])
    out[...] = total


def join_kernel(keep, came, grams, grams_came, acc, own, *rest, n_in):
    mine, grams_out, *give = rest[n_in:]
    width = own.shape[1]
    total = keep[0] + came[0].astype(F32) + own[...] + acc[0]
    for message in rest[:n_in]:
        total += message[:, :width].astype(F32)
    mine[...] = total
    total = grams[...] + grams_came[...]
    grams_out[...] = total
    for d in range(1, keep.shape[0]):
        give[d - 1][...] = pack((keep[d] + came[d].astype(F32)).astype(BF16), total)


def gather_sums(mine, grams, rest, n_in):
    image, total = mine[...], grams[...]
    width = image.shape[1]
    for message in rest[:n_in]:
        image += message[:, :width].astype(F32)
        total += unpack(message[...], width)
    return image, total, rest[n_in:]


def first_kernel(mine, grams, probes, *rest, n_in):
    image, total, (image_out, residual_out, rounded, totals, alpha_out) = gather_sums(
        mine, grams, rest, n_in
    )
    (alpha,) = eliminate([total])
    residual = probes[...] - dot32(alpha, image, TN)
    rounded[...] = residual.astype(BF16)
    residual_out[...] = residual
    image_out[...] = image
    totals[...] = total
    alpha_out[...] = alpha


def between_kernel(totals, alpha, probes, inverse_out, middle_out, solved_out):
    size = alpha.shape[0]
    eye = (
        lax.broadcasted_iota(jnp.int32, (size, size), 0)
        == lax.broadcasted_iota(jnp.int32, (size, size), 1)
    ).astype(F32)
    (inverse,) = eliminate([jnp.concatenate([totals[:, size:], eye], 1)])
    inverse_out[...] = inverse
    middle_out[...] = dot32(inverse, dot32(totals[:, :size], inverse, NN), TN)
    solved_out[...] = dot32(alpha[...], probes[...], TN)


def last_kernel(mine, grams, probes, image_in, residual_in, inverse, middle, solved, *rest, n_in):
    forward, total, (solution_out, residual_out) = gather_sums(mine, grams, rest, n_in)
    size = forward.shape[0]
    norm = total[:, size:]
    curv = total[:, :size] - dot32(norm, dot32(middle[...], norm, NN), TN)
    beta = dot32(inverse[...], norm, NN)
    residual = residual_in[...]
    direction = residual + dot32(beta, probes[...], TN)
    image = forward + dot32(beta, image_in[...], TN)
    (step,) = eliminate([jnp.concatenate([curv, norm], 1)])
    solution_out[...] = solved[...] + dot32(step, direction, TN)
    residual_out[...] = residual - dot32(step, image, TN)


def call(kernel, outs, args, specs=None, scratch=(), limit=32, name=None, work=None):
    return pl.pallas_call(
        kernel,
        out_shape=outs,
        in_specs=[VMEM] * len(args) if specs is None else specs,
        out_specs=[VMEM] * len(outs),
        scratch_shapes=list(scratch),
        compiler_params=pltpu.CompilerParams(vmem_limit_bytes=limit << 20),
        cost_estimate=None if work is None else pl.CostEstimate(flops=work, bytes_accessed=0, transcendentals=0),
        name=name,
    )(*args)


def body(n_row, n_col, tiles, diag_tiles, probes, rows_list, cols_list, counts):
    n_chip = n_col // 2
    p_size, width = probes.shape[1:]
    shape = jax.ShapeDtypeStruct
    block32 = shape((p_size, width), F32)
    block16 = shape((p_size, width), BF16)

    def over(value, axis, delta):
        size = n_row if axis == "row" else n_col
        return lax.ppermute(value, axis, [(i, i ^ delta) for i in range(size)])

    def over_chips(value):
        return [over(value, "col", 2 * d) for d in range(1, n_chip)]

    def over_rows(value):
        return [over(value, "row", d) for d in range(1, n_row)]

    apart = rows_list[0, 0] ^ lax.axis_index("col")
    index = jnp.concatenate(
        [counts[0], (apart % 2) * n_chip + apart // 2, cols_list[0, 0] ^ lax.axis_index("row")]
    )
    probes = probes[0]
    diag = diag_tiles[0]
    square = shape((p_size, 2 * p_size), F32)
    slots = tiles.shape[2]
    (held,) = call(
        load_kernel,
        [shape(tiles.shape[2:], BF16)],
        [index, tiles[0, 0]],
        [SMEM, ANY],
        [pltpu.SemaphoreType.DMA((slots,))],
        name="load",
    )
    passes = 2 * slots * p_size * width * width

    message = shape((p_size, width + 3 * p_size), BF16)

    def apply_operator(rounded, residual, held):
        *gathered, held = lax.optimization_barrier((*over_chips(rounded), *over_rows(rounded), held))
        far = [rounded, *gathered[n_chip - 1 :]]
        near_own = jnp.stack([rounded, *gathered[: n_chip - 1]])
        near_far = over(near_own, "col", 1)
        acc, own = call(
            mirrored_kernel,
            [shape((n_row, p_size, width), F32), block32],
            [index, near_own, near_far, held, diag],
            [SMEM] + [VMEM] * 4,
            [pltpu.VMEM((n_col, p_size, width), BF16)],
            name="mirrored",
            work=passes,
        )
        grams, *give_row = call(
            gram_kernel, [square] + [message] * (n_row - 1), [acc, own, residual, *far], name="gram"
        )
        from_rows = [over(block, "row", d + 1) for d, block in enumerate(give_row)]
        outs = [shape((n_chip, p_size, width), BF16), shape((n_chip, p_size, width), F32)]
        scratch = [pltpu.VMEM((n_row, p_size, width), BF16), pltpu.VMEM((n_col, p_size, width), F32)]
        give_core, keep = call(
            functools.partial(forward_kernel, n_row=n_row),
            outs,
            [index, held, grams, *far],
            [SMEM, VMEM, ANY] + [VMEM] * n_row,
            scratch,
            name="forward",
            work=passes,
        )
        give_core, *from_rows = lax.optimization_barrier((give_core, *from_rows))
        came = over(give_core, "col", 1)
        (grams,) = call(rows_kernel, [square], [grams, *from_rows], name="gram_rows")
        grams_came = over(grams, "col", 1)
        mine, grams, *give_chip = call(
            functools.partial(join_kernel, n_in=n_row - 1),
            [block32, square] + [message] * (n_chip - 1),
            [keep, came, grams, grams_came, acc, own, *from_rows],
            name="join",
        )
        return mine, grams, [over(block, "col", 2 * d + 2) for d, block in enumerate(give_chip)]

    small = shape((p_size, p_size), F32)
    mine, grams, parts = apply_operator(probes.astype(BF16), probes, held)
    image, residual, rounded, totals, alpha = call(
        functools.partial(first_kernel, n_in=n_chip - 1),
        [block32, block32, block16, square, small],
        [mine, grams, probes, *parts],
        name="first_step",
    )
    inverse, middle, solved = call(
        between_kernel, [small, small, block32], [totals, alpha, probes], name="between"
    )
    mine, grams, parts = apply_operator(rounded, residual, held)
    solved, residual = call(
        functools.partial(last_kernel, n_in=n_chip - 1),
        [block32, block32],
        [mine, grams, probes, image, residual, inverse, middle, solved, *parts],
        name="last_step",
    )
    return solved[None], residual[None]


def solution(mesh):
    placed = (
        P("row", "col", None, None, None),
        P(("row", "col"), None, None),
        P(("row", "col"), None, None),
        P("row", "col", None),
        P("row", "col", None),
        P("row", "col"),
    )
    return jax.shard_map(
        functools.partial(body, mesh.shape["row"], mesh.shape["col"]),
        mesh=mesh,
        in_specs=placed,
        out_specs=(P(("row", "col"), None, None), P(("row", "col"), None, None)),
        check_vma=False,
    )
```

```python
import functools

import jax
import jax.numpy as jnp
from jax import lax
from jax.experimental import pallas as pl
from jax.experimental.pallas import tpu as pltpu
from jax.sharding import PartitionSpec as P

ITERS = 2
F32 = jnp.float32
BF16 = jnp.bfloat16
HI = lax.Precision.HIGHEST
NT = (((1,), (1,)), ((), ()))
NN = (((1,), (0,)), ((), ()))
TN = (((0,), (0,)), ((), ()))
ANY = pl.BlockSpec(memory_space=pl.ANY)
VMEM = pl.BlockSpec(memory_space=pltpu.VMEM)
SMEM = pl.BlockSpec(memory_space=pltpu.SMEM)


def dot32(left, right, dims):
    return lax.dot_general(left, right, dims, precision=HI, preferred_element_type=F32)


def dot16(left, right, dims):
    return lax.dot_general(left, right, dims, preferred_element_type=F32)


def dot_exact16(left, right, dims):
    first = right.astype(BF16)
    rest = right - first.astype(F32)
    second = rest.astype(BF16)
    third = (rest - second.astype(F32)).astype(BF16)
    return dot16(left, first, dims) + (dot16(left, second, dims) + dot16(left, third, dims))


def eliminate(systems, group=8):
    size, width = systems[0].shape
    rows = lax.broadcasted_iota(jnp.int32, (size, width), 0)
    for start in range(0, size, group):
        after = []
        for system in systems:
            columns = [
                jnp.broadcast_to(system[:, k : k + 1], (size, width)) for k in range(start, start + group)
            ]
            for place, k in enumerate(range(start, start + group)):
                inverse = 1.0 / columns[place][k : k + 1, :]
                here = rows == k
                scaled = system[k : k + 1, :] * inverse
                for later in range(place + 1, group):
                    factor = columns[later][k : k + 1, :] * inverse
                    columns[later] = jnp.where(here, factor, columns[later] - columns[place] * factor)
                system = jnp.where(here, scaled, system - columns[place] * scaled)
            after.append(system)
        systems = after
    return [system[:, size:] for system in systems]


def split16(value):
    first = value.astype(BF16)
    return first, (value - first.astype(F32)).astype(BF16)


def pack(block, grams):
    size = grams.shape[0]
    rows = lax.broadcasted_iota(jnp.int32, (size, size), 0)
    columns = lax.broadcasted_iota(jnp.int32, (size, size), 1)
    both = jnp.where(rows >= columns, grams[:, :size], grams[:, size:])
    diagonal = jnp.sum(jnp.where(rows == columns, grams[:, size:], 0.0), axis=1, keepdims=True)
    first, second = split16(both)
    top, rest = split16(jnp.broadcast_to(diagonal, (size, size)))
    return jnp.concatenate([block, first, second, jnp.where(columns == 0, top, rest)], 1)


def unpack(message, width):
    size = message.shape[0]
    parts = message[:, width:].astype(F32)
    both = parts[:, :size] + parts[:, size : 2 * size]
    diagonal = parts[:, 2 * size : 2 * size + 1] + parts[:, 2 * size + 1 : 2 * size + 2]
    rows = lax.broadcasted_iota(jnp.int32, (size, size), 0)
    columns = lax.broadcasted_iota(jnp.int32, (size, size), 1)
    turned = both.T
    first = jnp.where(rows >= columns, both, turned)
    second = jnp.where(rows < columns, both, turned)
    return jnp.concatenate([first, jnp.where(rows == columns, diagonal, second)], 1)


def held_slots(count, slots, work, ready=None):
    group = 4 if slots % 4 == 0 else 1

    def turn(g, carry):
        if ready is not None:
            for u in range(group):
                pl.when(g * group + u < count)(functools.partial(ready, g * group + u))
        for u in range(group):
            work(g * group + u, g * group + u < count)
        return carry

    lax.fori_loop(0, (count + group - 1) // group, turn, 0)


def forward_products(index, tiles, far_in, give_core, acc, own, far, ready=None):
    n_chip = give_core.shape[0]
    slots = tiles.shape[0] - 1
    for d, block in enumerate(far_in):
        far[d] = block[...]
    acc[...] = jnp.zeros_like(acc)

    def work(slot, held):
        i = index[1 + slot]
        j = index[1 + slots + slot]
        acc[i] += jnp.where(held, dot16(far[j], tiles[slot], NT), 0.0)

    held_slots(index[0], slots, work, ready)
    if ready is not None:
        ready(slots)
    own[...] = dot16(far[0], tiles[slots], NT)
    for d in range(n_chip):
        give_core[d] = acc[n_chip + d].astype(BF16)


def forward_kernel(index, tiles, *rest, n_row):
    give_core, acc, own, far = rest[n_row:]
    forward_products(index, tiles, rest[:n_row], give_core, acc, own, far)


def forward_load_kernel(index, diag, stored, *rest, n_row):
    give_core, acc, own, tiles, far, arrived = rest[n_row:]
    slots = stored.shape[0]

    def fetch(slot):
        return pltpu.make_async_copy(stored.at[slot], tiles.at[slot], arrived.at[slot])

    last = pltpu.make_async_copy(diag, tiles.at[slots], arrived.at[slots])

    def ready(slot):
        if isinstance(slot, int):
            last.wait()
        else:
            fetch(slot).wait()

    def begin(slot, carry):
        fetch(slot).start()
        return carry

    lax.fori_loop(0, index[0], begin, 0)
    last.start()
    forward_products(index, tiles, rest[:n_row], give_core, acc, own, far, ready)


def gram_kernel(acc, came, own, residual, *rest):
    *near, keep, grams = rest
    size = own.shape[0]
    half = 0.5 * dot_exact16(near[0][...], own[...], NT)
    for d, block in enumerate(near):
        both = acc[d] + came[d].astype(F32)
        keep[d] = both
        half += dot_exact16(block[...], both, NT)
    grams[:, :size] = half + half.T
    grams[:, size:] = dot32(residual[...], residual[...], NT)


def mirrored_kernel(index, near_own, near_far, tiles, acc, near):
    n_chip = near_own.shape[0]
    slots = tiles.shape[0] - 1
    for d in range(n_chip):
        near[d] = near_own[d]
        near[n_chip + d] = near_far[d]
    acc[...] = jnp.zeros_like(acc)

    def work(slot, held):
        i = index[1 + slot]
        j = index[1 + slots + slot]
        acc[j] += jnp.where(held, dot16(near[i], tiles[slot], NN), 0.0)

    held_slots(index[0], slots, work)


def join_kernel(keep, grams, grams_came, grams_out, *give):
    total = grams[...] + grams_came[...]
    grams_out[...] = total
    for d in range(1, keep.shape[0]):
        give[d - 1][...] = pack(keep[d].astype(BF16), total)


def rows_kernel(keep, grams, own, acc, *rest, n_in):
    image, total, (mine_out, grams_out, *give) = gather_sums(keep[0], grams[...], rest, n_in)
    mine_out[...] = image + own[...] + acc[0]
    grams_out[...] = total
    for d in range(1, acc.shape[0]):
        give[d - 1][...] = pack(acc[d].astype(BF16), total)


def gather_sums(mine, grams, rest, n_in):
    image, total = mine, grams
    width = image.shape[1]
    for message in rest[:n_in]:
        image += message[:, :width].astype(F32)
        total += unpack(message[...], width)
    return image, total, rest[n_in:]


def first_kernel(mine, grams, probes, *rest, n_in):
    image, total, (image_out, residual_out, rounded, totals, alpha_out) = gather_sums(
        mine[...], grams[...], rest, n_in
    )
    (alpha,) = eliminate([total])
    residual = probes[...] - dot32(alpha, image, TN)
    rounded[...] = residual.astype(BF16)
    residual_out[...] = residual
    image_out[...] = image
    totals[...] = total
    alpha_out[...] = alpha


def between_kernel(totals, alpha, probes, inverse_out, middle_out, solved_out):
    size = alpha.shape[0]
    eye = (
        lax.broadcasted_iota(jnp.int32, (size, size), 0)
        == lax.broadcasted_iota(jnp.int32, (size, size), 1)
    ).astype(F32)
    (inverse,) = eliminate([jnp.concatenate([totals[:, size:], eye], 1)])
    inverse_out[...] = inverse
    middle_out[...] = dot32(inverse, dot32(totals[:, :size], inverse, NN), TN)
    solved_out[...] = dot32(alpha[...], probes[...], TN)


def last_kernel(mine, grams, probes, image_in, residual_in, inverse, middle, solved, *rest, n_in):
    forward, total, (solution_out, residual_out) = gather_sums(mine[...], grams[...], rest, n_in)
    size = forward.shape[0]
    norm = total[:, size:]
    curv = total[:, :size] - dot32(norm, dot32(middle[...], norm, NN), TN)
    beta = dot32(inverse[...], norm, NN)
    residual = residual_in[...]
    direction = residual + dot32(beta, probes[...], TN)
    image = forward + dot32(beta, image_in[...], TN)
    (step,) = eliminate([jnp.concatenate([curv, norm], 1)])
    solution_out[...] = solved[...] + dot32(step, direction, TN)
    residual_out[...] = residual - dot32(step, image, TN)


def call(kernel, outs, args, specs=None, scratch=(), limit=32, name=None, work=None):
    return pl.pallas_call(
        kernel,
        out_shape=outs,
        in_specs=[VMEM] * len(args) if specs is None else specs,
        out_specs=[VMEM] * len(outs),
        scratch_shapes=list(scratch),
        compiler_params=pltpu.CompilerParams(vmem_limit_bytes=limit << 20),
        cost_estimate=None if work is None else pl.CostEstimate(flops=work, bytes_accessed=0, transcendentals=0),
        name=name,
    )(*args)


def body(n_row, n_col, tiles, diag_tiles, probes, rows_list, cols_list, counts):
    n_chip = n_col // 2
    p_size, width = probes.shape[1:]
    shape = jax.ShapeDtypeStruct
    block32 = shape((p_size, width), F32)
    block16 = shape((p_size, width), BF16)

    def over(value, axis, delta):
        size = n_row if axis == "row" else n_col
        return lax.ppermute(value, axis, [(i, i ^ delta) for i in range(size)])

    def over_chips(value):
        return [over(value, "col", 2 * d) for d in range(1, n_chip)]

    def over_rows(value):
        return [over(value, "row", d) for d in range(1, n_row)]

    apart = rows_list[0, 0] ^ lax.axis_index("col")
    index = jnp.concatenate(
        [counts[0], (apart % 2) * n_chip + apart // 2, cols_list[0, 0] ^ lax.axis_index("row")]
    )
    probes = probes[0]
    diag = diag_tiles[0]
    square = shape((p_size, 2 * p_size), F32)
    slots = tiles.shape[2]
    passes = 2 * slots * p_size * width * width

    message = shape((p_size, width + 3 * p_size), BF16)

    def apply_operator(rounded, residual, held=None):
        from_rows = over_rows(rounded)
        near = over_chips(rounded)
        outs = [shape((n_chip, p_size, width), BF16), shape((n_col, p_size, width), F32), block32]
        scratch = [pltpu.VMEM((n_row, p_size, width), BF16)]
        if held is None:
            give_core, acc_row, own, held = call(
                functools.partial(forward_load_kernel, n_row=n_row),
                outs + [shape((slots + 1, width, width), BF16)],
                [index, diag, tiles[0, 0], rounded, *from_rows],
                [SMEM, ANY, ANY] + [VMEM] * n_row,
                scratch + [pltpu.SemaphoreType.DMA((slots + 1,))],
                name="forward_load",
                work=1,
            )
        else:
            give_core, acc_row, own = call(
                functools.partial(forward_kernel, n_row=n_row),
                outs,
                [index, held, rounded, *from_rows],
                [SMEM] + [VMEM] * (1 + n_row),
                scratch,
                name="forward",
                work=1,
            )
        give_core, *near = lax.optimization_barrier((give_core, *near))
        came = over(give_core, "col", 1)
        near_own = jnp.stack([rounded, *near])
        near_far = over(near_own, "col", 1)
        keep, grams = call(
            gram_kernel,
            [shape((n_chip, p_size, width), F32), square],
            [acc_row, came, own, residual, rounded, *near],
            name="gram",
        )
        grams_came = over(grams, "col", 1)
        grams, *give = call(
            join_kernel, [square] + [message] * (n_chip - 1), [keep, grams, grams_came], name="join"
        )
        parts = [over(block, "col", 2 * d + 2) for d, block in enumerate(give)]
        (acc_col,) = call(
            mirrored_kernel,
            [shape((n_row, p_size, width), F32)],
            [index, near_own, near_far, held],
            [SMEM] + [VMEM] * 3,
            [pltpu.VMEM((n_col, p_size, width), BF16)],
            name="mirrored",
            work=passes,
        )
        mine, grams, *give = call(
            functools.partial(rows_kernel, n_in=n_chip - 1),
            [block32, square] + [message] * (n_row - 1),
            [keep, grams, own, acc_col, *parts],
            name="rows",
        )
        return mine, grams, [over(block, "row", d + 1) for d, block in enumerate(give)], held

    small = shape((p_size, p_size), F32)
    mine, grams, parts, held = apply_operator(probes.astype(BF16), probes)
    image, residual, rounded, totals, alpha = call(
        functools.partial(first_kernel, n_in=n_row - 1),
        [block32, block32, block16, square, small],
        [mine, grams, probes, *parts],
        name="first_step",
    )
    inverse, middle, solved = call(
        between_kernel, [small, small, block32], [totals, alpha, probes], name="between"
    )
    mine, grams, parts, held = apply_operator(rounded, residual, held)
    solved, residual = call(
        functools.partial(last_kernel, n_in=n_row - 1),
        [block32, block32],
        [mine, grams, probes, image, residual, inverse, middle, solved, *parts],
        name="last_step",
    )
    return solved[None], residual[None]


def solution(mesh):
    placed = (
        P("row", "col", None, None, None),
        P(("row", "col"), None, None),
        P(("row", "col"), None, None),
        P("row", "col", None),
        P("row", "col", None),
        P("row", "col"),
    )
    return jax.shard_map(
        functools.partial(body, mesh.shape["row"], mesh.shape["col"]),
        mesh=mesh,
        in_specs=placed,
        out_specs=(P(("row", "col"), None, None), P(("row", "col"), None, None)),
        check_vma=False,
    )
```

```python
import functools

import jax
import jax.numpy as jnp
from jax import lax
from jax.experimental import pallas as pl
from jax.experimental.pallas import tpu as pltpu
from jax.sharding import PartitionSpec as P

START = 10**10
F32 = jnp.float32
BF16 = jnp.bfloat16
HI = lax.Precision.HIGHEST
NT = (((1,), (1,)), ((), ()))
NN = (((1,), (0,)), ((), ()))
TN = (((0,), (0,)), ((), ()))
VMEM = pl.BlockSpec(memory_space=pltpu.VMEM)
SMEM = pl.BlockSpec(memory_space=pltpu.SMEM)


def dot32(left, right, dims):
    return lax.dot_general(left, right, dims, precision=HI, preferred_element_type=F32)


def dot16(left, right, dims):
    return lax.dot_general(left, right, dims, preferred_element_type=F32)


def dot_exact16(left, right, dims):
    first = right.astype(BF16)
    rest = right - first.astype(F32)
    second = rest.astype(BF16)
    third = (rest - second.astype(F32)).astype(BF16)
    return dot16(left, first, dims) + (dot16(left, second, dims) + dot16(left, third, dims))


def eliminate(systems, group=8):
    size, width = systems[0].shape
    rows = lax.broadcasted_iota(jnp.int32, (size, width), 0)
    for start in range(0, size, group):
        after = []
        for system in systems:
            columns = [
                jnp.broadcast_to(system[:, k : k + 1], (size, width)) for k in range(start, start + group)
            ]
            for place, k in enumerate(range(start, start + group)):
                inverse = 1.0 / columns[place][k : k + 1, :]
                here = rows == k
                scaled = system[k : k + 1, :] * inverse
                for later in range(place + 1, group):
                    factor = columns[later][k : k + 1, :] * inverse
                    columns[later] = jnp.where(here, factor, columns[later] - columns[place] * factor)
                system = jnp.where(here, scaled, system - columns[place] * scaled)
            after.append(system)
        systems = after
    return [system[:, size:] for system in systems]


def split16(value):
    first = value.astype(BF16)
    return first, (value - first.astype(F32)).astype(BF16)


def pack(block, grams):
    size = grams.shape[0]
    rows = lax.broadcasted_iota(jnp.int32, (size, size), 0)
    columns = lax.broadcasted_iota(jnp.int32, (size, size), 1)
    both = jnp.where(rows >= columns, grams[:, :size], grams[:, size:])
    diagonal = jnp.sum(jnp.where(rows == columns, grams[:, size:], 0.0), axis=1, keepdims=True)
    first, second = split16(both)
    top, rest = split16(jnp.broadcast_to(diagonal, (size, size)))
    return jnp.concatenate([block, first, second, jnp.where(columns == 0, top, rest)], 1)


def unpack(message, width):
    size = message.shape[0]
    parts = message[:, width:].astype(F32)
    both = parts[:, :size] + parts[:, size : 2 * size]
    diagonal = parts[:, 2 * size : 2 * size + 1] + parts[:, 2 * size + 1 : 2 * size + 2]
    rows = lax.broadcasted_iota(jnp.int32, (size, size), 0)
    columns = lax.broadcasted_iota(jnp.int32, (size, size), 1)
    turned = both.T
    first = jnp.where(rows >= columns, both, turned)
    second = jnp.where(rows < columns, both, turned)
    return jnp.concatenate([first, jnp.where(rows == columns, diagonal, second)], 1)


def held_slots(count, slots, work):
    group = 4 if slots % 4 == 0 else 1

    def turn(g, carry):
        for u in range(group):
            work(g * group + u, g * group + u < count)
        return carry

    lax.fori_loop(0, (count + group - 1) // group, turn, 0)


def places(index, slots, n_row, n_chip):
    row, column = lax.axis_index("row"), lax.axis_index("col")

    def place(slot):
        apart = index[1 + slot] ^ column
        return (apart % 2) * n_chip + apart // 2, index[1 + slots + slot] ^ row

    return place


def round_kernel(value, out):
    out[...] = value[...].astype(BF16)


def forward_kernel(index, tiles, *rest, n_row):
    far_in = rest[:n_row]
    give_core, acc, far = rest[n_row:]
    n_chip = give_core.shape[0]
    slots = tiles.shape[0]
    place = places(index, slots, n_row, n_chip)
    for d, block in enumerate(far_in):
        far[d] = block[...]
    acc[...] = jnp.zeros_like(acc)

    def work(slot, held):
        i, j = place(slot)
        acc[i] += jnp.where(held, dot16(far[j], tiles[slot], NT), 0.0)

    held_slots(index[0], slots, work)
    for d in range(n_chip):
        give_core[d] = acc[n_chip + d].astype(BF16)


def gram_kernel(acc, came, diag, residual, *rest):
    *near, keep, own_out, grams = rest
    size = residual.shape[0]
    own = dot16(near[0][...], diag[...], NT)
    own_out[...] = own
    half = 0.5 * dot_exact16(near[0][...], own, NT)
    for d, block in enumerate(near):
        both = acc[d] + came[d].astype(F32)
        keep[d] = both
        half += dot_exact16(block[...], both, NT)
    grams[:, :size] = half + half.T
    grams[:, size:] = dot32(residual[...], residual[...], NT)


def mirrored_kernel(index, near_own, near_far, tiles, acc, near):
    n_chip = near_own.shape[0]
    slots = tiles.shape[0]
    place = places(index, slots, acc.shape[0], n_chip)
    for d in range(n_chip):
        near[d] = near_own[d]
        near[n_chip + d] = near_far[d]
    acc[...] = jnp.zeros_like(acc)

    def work(slot, held):
        i, j = place(slot)
        acc[j] += jnp.where(held, dot16(near[i], tiles[slot], NN), 0.0)

    held_slots(index[0], slots, work)


def join_kernel(keep, grams, grams_came, grams_out, *give):
    total = grams[...] + grams_came[...]
    grams_out[...] = total
    for d in range(1, keep.shape[0]):
        give[d - 1][...] = pack(keep[d].astype(BF16), total)


def rows_kernel(keep, grams, own, acc, *rest, n_in):
    image, total, (mine_out, grams_out, *give) = gather_sums(keep[0], grams[...], rest, n_in)
    mine_out[...] = image + own[...] + acc[0]
    grams_out[...] = total
    for d in range(1, acc.shape[0]):
        give[d - 1][...] = pack(acc[d].astype(BF16), total)


def gather_sums(mine, grams, rest, n_in):
    image, total = mine, grams
    width = image.shape[1]
    for message in rest[:n_in]:
        image += message[:, :width].astype(F32)
        total += unpack(message[...], width)
    return image, total, rest[n_in:]


def first_kernel(mine, grams, probes, *rest, n_in):
    image, total, (image_out, residual_out, rounded, totals, alpha_out) = gather_sums(
        mine[...], grams[...], rest, n_in
    )
    (alpha,) = eliminate([total])
    residual = probes[...] - dot32(alpha, image, TN)
    rounded[...] = residual.astype(BF16)
    residual_out[...] = residual
    image_out[...] = image
    totals[...] = total
    alpha_out[...] = alpha


def between_kernel(totals, alpha, probes, inverse_out, middle_out, solved_out):
    size = alpha.shape[0]
    eye = (
        lax.broadcasted_iota(jnp.int32, (size, size), 0)
        == lax.broadcasted_iota(jnp.int32, (size, size), 1)
    ).astype(F32)
    (inverse,) = eliminate([jnp.concatenate([totals[:, size:], eye], 1)])
    inverse_out[...] = inverse
    middle_out[...] = dot32(inverse, dot32(totals[:, :size], inverse, NN), TN)
    solved_out[...] = dot32(alpha[...], probes[...], TN)


def last_kernel(mine, grams, probes, image_in, residual_in, inverse, middle, solved, *rest, n_in):
    forward, total, (solution_out, residual_out) = gather_sums(mine[...], grams[...], rest, n_in)
    size = forward.shape[0]
    norm = total[:, size:]
    curv = total[:, :size] - dot32(norm, dot32(middle[...], norm, NN), TN)
    beta = dot32(inverse[...], norm, NN)
    residual = residual_in[...]
    direction = residual + dot32(beta, probes[...], TN)
    image = forward + dot32(beta, image_in[...], TN)
    (step,) = eliminate([jnp.concatenate([curv, norm], 1)])
    solution_out[...] = solved[...] + dot32(step, direction, TN)
    residual_out[...] = residual - dot32(step, image, TN)


def call(kernel, outs, args, specs=None, scratch=(), limit=32, name=None, work=None):
    return pl.pallas_call(
        kernel,
        out_shape=outs,
        in_specs=[VMEM] * len(args) if specs is None else specs,
        out_specs=[VMEM] * len(outs),
        scratch_shapes=list(scratch),
        compiler_params=pltpu.CompilerParams(vmem_limit_bytes=limit << 20),
        cost_estimate=None if work is None else pl.CostEstimate(flops=work, bytes_accessed=0, transcendentals=0),
        name=name,
    )(*args)


def body(n_row, n_col, tiles, diag_tiles, probes, rows_list, cols_list, counts):
    n_chip = n_col // 2
    p_size, width = probes.shape[1:]
    shape = jax.ShapeDtypeStruct
    block32 = shape((p_size, width), F32)
    block16 = shape((p_size, width), BF16)

    def over(value, axis, delta):
        size = n_row if axis == "row" else n_col
        return lax.ppermute(value, axis, [(i, i ^ delta) for i in range(size)])

    def over_chips(value):
        return [over(value, "col", 2 * d) for d in range(1, n_chip)]

    def over_rows(value):
        return [over(value, "row", d) for d in range(1, n_row)]

    index = jnp.concatenate([counts[0], rows_list[0, 0], cols_list[0, 0]])
    probes = probes[0]
    diag = diag_tiles[0]
    held = tiles[0, 0]
    square = shape((p_size, 2 * p_size), F32)
    slots = tiles.shape[2]
    passes = 2 * slots * p_size * width * width

    message = shape((p_size, width + 3 * p_size), BF16)

    def apply_operator(rounded, residual):
        from_rows = over_rows(rounded)
        near = over_chips(rounded)
        give_core, acc_row = call(
            functools.partial(forward_kernel, n_row=n_row),
            [shape((n_chip, p_size, width), BF16), shape((n_col, p_size, width), F32)],
            [index, held, rounded, *from_rows],
            [SMEM] + [VMEM] * (1 + n_row),
            [pltpu.VMEM((n_row, p_size, width), BF16)],
            name="forward",
            work=1,
        )
        give_core, *near = lax.optimization_barrier((give_core, *near))
        came = over(give_core, "col", 1)
        near_own = jnp.stack([rounded, *near])
        near_far = over(near_own, "col", 1)
        keep, own, grams = call(
            gram_kernel,
            [shape((n_chip, p_size, width), F32), block32, square],
            [acc_row, came, diag, residual, rounded, *near],
            name="gram",
        )
        grams_came = over(grams, "col", 1)
        grams, *give = call(
            join_kernel, [square] + [message] * (n_chip - 1), [keep, grams, grams_came], name="join"
        )
        parts = [over(block, "col", 2 * d + 2) for d, block in enumerate(give)]
        (acc_col,) = call(
            mirrored_kernel,
            [shape((n_row, p_size, width), F32)],
            [index, near_own, near_far, held],
            [SMEM] + [VMEM] * 3,
            [pltpu.VMEM((n_col, p_size, width), BF16)],
            name="mirrored",
            work=passes,
        )
        mine, grams, *give = call(
            functools.partial(rows_kernel, n_in=n_chip - 1),
            [block32, square] + [message] * (n_row - 1),
            [keep, grams, own, acc_col, *parts],
            name="rows",
        )
        return mine, grams, [over(block, "row", d + 1) for d, block in enumerate(give)]

    small = shape((p_size, p_size), F32)
    (rounded,) = call(round_kernel, [block16], [probes], name="round", work=START)
    mine, grams, parts = apply_operator(rounded, probes)
    image, residual, rounded, totals, alpha = call(
        functools.partial(first_kernel, n_in=n_row - 1),
        [block32, block32, block16, square, small],
        [mine, grams, probes, *parts],
        name="first_step",
    )
    inverse, middle, solved = call(
        between_kernel, [small, small, block32], [totals, alpha, probes], name="between"
    )
    mine, grams, parts = apply_operator(rounded, residual)
    solved, residual = call(
        functools.partial(last_kernel, n_in=n_row - 1),
        [block32, block32],
        [mine, grams, probes, image, residual, inverse, middle, solved, *parts],
        name="last_step",
    )
    return solved[None], residual[None]


def solution(mesh):
    placed = (
        P("row", "col", None, None, None),
        P(("row", "col"), None, None),
        P(("row", "col"), None, None),
        P("row", "col", None),
        P("row", "col", None),
        P("row", "col"),
    )
    return jax.shard_map(
        functools.partial(body, mesh.shape["row"], mesh.shape["col"]),
        mesh=mesh,
        in_specs=placed,
        out_specs=(P(("row", "col"), None, None), P(("row", "col"), None, None)),
        check_vma=False,
    )
```

```python
import functools

import jax
import jax.numpy as jnp
from jax import lax
from jax.experimental import pallas as pl
from jax.experimental.pallas import tpu as pltpu
from jax.sharding import PartitionSpec as P

START = 10**10
F32 = jnp.float32
BF16 = jnp.bfloat16
HI = lax.Precision.HIGHEST
NT = (((1,), (1,)), ((), ()))
NN = (((1,), (0,)), ((), ()))
TN = (((0,), (0,)), ((), ()))
ANY = pl.BlockSpec(memory_space=pl.ANY)
VMEM = pl.BlockSpec(memory_space=pltpu.VMEM)
SMEM = pl.BlockSpec(memory_space=pltpu.SMEM)


def dot32(left, right, dims):
    return lax.dot_general(left, right, dims, precision=HI, preferred_element_type=F32)


def dot16(left, right, dims):
    return lax.dot_general(left, right, dims, preferred_element_type=F32)


def dot_exact16(left, right, dims):
    first = right.astype(BF16)
    rest = right - first.astype(F32)
    second = rest.astype(BF16)
    third = (rest - second.astype(F32)).astype(BF16)
    return dot16(left, first, dims) + (dot16(left, second, dims) + dot16(left, third, dims))


def eliminate(systems, group=16):
    size, width = systems[0].shape
    rows = lax.broadcasted_iota(jnp.int32, (size, width), 0)
    for start in range(0, size, group):
        after = []
        for system in systems:
            columns = [
                jnp.broadcast_to(system[:, k : k + 1], (size, width)) for k in range(start, start + group)
            ]
            for place, k in enumerate(range(start, start + group)):
                inverse = 1.0 / columns[place][k : k + 1, :]
                here = rows == k
                scaled = system[k : k + 1, :] * inverse
                for later in range(place + 1, group):
                    factor = columns[later][k : k + 1, :] * inverse
                    columns[later] = jnp.where(here, factor, columns[later] - columns[place] * factor)
                system = jnp.where(here, scaled, system - columns[place] * scaled)
            after.append(system)
        systems = after
    return [system[:, size:] for system in systems]


def split16(value):
    first = value.astype(BF16)
    return first, (value - first.astype(F32)).astype(BF16)


def compact(block):
    size, width = block.shape
    whole = width - width % 128
    rows = [block[:, at : at + 128] for at in range(0, whole, 128)]
    if whole < width:
        each = size * (width - whole) // 128
        tail = [block[at : at + each, whole:] for at in range(0, size, each)]
        rows.append(jnp.concatenate(tail, 1))
    return jnp.concatenate(rows, 0)


def spread(rows, size):
    width = rows.shape[0] * 128 // size
    whole, rest = width // 128, width % 128
    columns = [rows[k * size : (k + 1) * size] for k in range(whole)]
    if rest:
        tail = rows[whole * size :]
        columns.append(jnp.concatenate([tail[:, at : at + rest] for at in range(0, 128, rest)], 0))
    return jnp.concatenate(columns, 1)


def pack(block, grams):
    size = grams.shape[0]
    rows = lax.broadcasted_iota(jnp.int32, (size, size), 0)
    columns = lax.broadcasted_iota(jnp.int32, (size, size), 1)
    both = jnp.where(rows >= columns, grams[:, :size], grams[:, size:])
    diagonal = jnp.sum(jnp.where(rows == columns, grams[:, size:], 0.0), axis=0, keepdims=True)
    parts = jnp.concatenate(split16(both), 1)
    last = jnp.concatenate(split16(jnp.broadcast_to(diagonal, (16, size))), 1)
    return jnp.concatenate([compact(block), parts, last], 0)


def unpack(message, size):
    end = message.shape[0]
    parts = message[end - 16 - size : end - 16].astype(F32)
    last = message[end - 16 :].astype(F32)
    both = parts[:, :size] + parts[:, size:]
    diagonal = (last[:, :size] + last[:, size:])[:1]
    rows = lax.broadcasted_iota(jnp.int32, (size, size), 0)
    columns = lax.broadcasted_iota(jnp.int32, (size, size), 1)
    turned = both.T
    first = jnp.where(rows >= columns, both, turned)
    second = jnp.where(rows < columns, both, turned)
    second = jnp.where(rows == columns, diagonal, second)
    return spread(message[: end - 16 - size], size).astype(F32), jnp.concatenate([first, second], 1)


def held_slots(count, slots, work):
    group = 4 if slots % 4 == 0 else 1

    def turn(g, carry):
        for u in range(group):
            work(g * group + u, g * group + u < count)
        return carry

    lax.fori_loop(0, (count + group - 1) // group, turn, 0)


def places(index, slots, n_row, n_chip):
    row, column = lax.axis_index("row"), lax.axis_index("col")

    def place(slot):
        apart = index[1 + slot] ^ column
        return (apart % 2) * n_chip + apart // 2, index[1 + slots + slot] ^ row

    return place


def round_kernel(value, out):
    out[...] = compact(value[...].astype(BF16))


def forward_kernel(index, tiles, after, *rest, n_row):
    far_in = rest[:n_row]
    give_core, acc, far = rest[n_row:]
    n_chip = give_core.shape[0]
    slots = tiles.shape[0]
    place = places(index, slots, n_row, n_chip)
    for d, block in enumerate(far_in):
        far[d] = spread(block[...], far.shape[1])
    acc[...] = jnp.zeros_like(acc)

    def work(slot, held):
        i, j = place(slot)
        acc[i] += jnp.where(held, dot16(far[j], tiles[slot], NT), 0.0)

    held_slots(index[0], slots, work)
    for d in range(n_chip):
        give_core[d] = acc[n_chip + d].astype(BF16)


def own_kernel(near, diag, residual, own_out, grams):
    size = residual.shape[0]
    block = spread(near[...], size)
    own = dot16(block, diag[...], NT)
    own_out[...] = own
    half = 0.5 * dot_exact16(block, own, NT)
    grams[:, :size] = half + half.T
    grams[:, size:] = dot32(residual[...], residual[...], NT)


def gram_kernel(acc, came, grams_own, *rest):
    *near, keep, grams = rest
    size = grams.shape[0]
    half = jnp.zeros((size, size), F32)
    for d, block in enumerate(near):
        both = acc[d] + came[d].astype(F32)
        keep[d] = both
        half += dot_exact16(spread(block[...], size), both, NT)
    grams[:, :size] = grams_own[:, :size] + half + half.T
    grams[:, size:] = grams_own[:, size:]


def mirrored_kernel(index, near_own, near_far, tiles, acc, near):
    n_chip = near_own.shape[0]
    slots = tiles.shape[0]
    place = places(index, slots, acc.shape[0], n_chip)
    for d in range(n_chip):
        near[d] = spread(near_own[d], near.shape[1])
        near[n_chip + d] = spread(near_far[d], near.shape[1])
    acc[...] = jnp.zeros_like(acc)

    def work(slot, held):
        i, j = place(slot)
        acc[j] += jnp.where(held, dot16(near[i], tiles[slot], NN), 0.0)

    held_slots(index[0], slots, work)


def join_kernel(keep, grams, grams_came, grams_out, *give):
    total = grams[...] + grams_came[...]
    grams_out[...] = total
    for d in range(1, keep.shape[0]):
        give[d - 1][...] = pack(keep[d].astype(BF16), total)


def rows_kernel(keep, grams, own, acc, *rest, n_in):
    image, total, (mine_out, grams_out, *give) = gather_sums(keep[0], grams[...], rest, n_in)
    mine_out[...] = image + own[...] + acc[0]
    grams_out[...] = total
    for d in range(1, acc.shape[0]):
        give[d - 1][...] = pack(acc[d].astype(BF16), total)


def gather_sums(mine, grams, rest, n_in):
    image, total = mine, grams
    for message in rest[:n_in]:
        block, matrices = unpack(message[...], image.shape[0])
        image += block
        total += matrices
    return image, total, rest[n_in:]


def first_kernel(mine, grams, probes, *rest, n_in):
    image, total, (image_out, residual_out, rounded, totals, alpha_out) = gather_sums(
        mine[...], grams[...], rest, n_in
    )
    (alpha,) = eliminate([total])
    residual = probes[...] - dot32(alpha, image, TN)
    rounded[...] = compact(residual.astype(BF16))
    residual_out[...] = residual
    image_out[...] = image
    totals[...] = total
    alpha_out[...] = alpha


def between_kernel(totals, alpha, probes, inverse_out, middle_out, solved_out):
    size = alpha.shape[0]
    eye = (
        lax.broadcasted_iota(jnp.int32, (size, size), 0)
        == lax.broadcasted_iota(jnp.int32, (size, size), 1)
    ).astype(F32)
    (inverse,) = eliminate([jnp.concatenate([totals[:, size:], eye], 1)])
    inverse_out[...] = inverse
    middle_out[...] = dot32(inverse, dot32(totals[:, :size], inverse, NN), TN)
    solved_out[...] = dot32(alpha[...], probes[...], TN)


def last_kernel(mine, grams, probes, image_in, residual_in, inverse, middle, solved, *rest, n_in):
    forward, total, (solution_out, residual_out) = gather_sums(mine[...], grams[...], rest, n_in)
    size = forward.shape[0]
    norm = total[:, size:]
    curv = total[:, :size] - dot32(norm, dot32(middle[...], norm, NN), TN)
    beta = dot32(inverse[...], norm, NN)
    residual = residual_in[...]
    direction = residual + dot32(beta, probes[...], TN)
    image = forward + dot32(beta, image_in[...], TN)
    (step,) = eliminate([jnp.concatenate([curv, norm], 1)])
    solution_out[...] = solved[...] + dot32(step, direction, TN)
    residual_out[...] = residual - dot32(step, image, TN)


def call(kernel, outs, args, specs=None, scratch=(), limit=32, name=None, work=None):
    return pl.pallas_call(
        kernel,
        out_shape=outs,
        in_specs=[VMEM] * len(args) if specs is None else specs,
        out_specs=[VMEM] * len(outs),
        scratch_shapes=list(scratch),
        compiler_params=pltpu.CompilerParams(vmem_limit_bytes=limit << 20),
        cost_estimate=None if work is None else pl.CostEstimate(flops=work, bytes_accessed=0, transcendentals=0),
        name=name,
    )(*args)


def body(n_row, n_col, tiles, diag_tiles, probes, rows_list, cols_list, counts):
    n_chip = n_col // 2
    p_size, width = probes.shape[1:]
    shape = jax.ShapeDtypeStruct
    block32 = shape((p_size, width), F32)
    block16 = shape((p_size * width // 128, 128), BF16)

    def over(value, axis, delta):
        size = n_row if axis == "row" else n_col
        return lax.ppermute(value, axis, [(i, i ^ delta) for i in range(size)])

    def over_chips(value):
        return [over(value, "col", 2 * d) for d in range(1, n_chip)]

    def over_rows(value):
        return [over(value, "row", d) for d in range(1, n_row)]

    index = jnp.concatenate([counts[0], rows_list[0, 0], cols_list[0, 0]])
    probes = probes[0]
    diag = diag_tiles[0]
    held = tiles[0, 0]
    square = shape((p_size, 2 * p_size), F32)
    slots = tiles.shape[2]
    passes = 2 * slots * p_size * width * width

    message = shape((block16.shape[0] + p_size + 16, 128), BF16)

    def apply_operator(rounded, residual):
        from_rows = over_rows(rounded)
        near = over_chips(rounded)
        own, grams = call(own_kernel, [block32, square], [rounded, diag, residual], name="own")
        give_core, acc_row = call(
            functools.partial(forward_kernel, n_row=n_row),
            [shape((n_chip, p_size, width), BF16), shape((n_col, p_size, width), F32)],
            [index, held, grams, rounded, *from_rows],
            [SMEM, VMEM, ANY] + [VMEM] * n_row,
            [pltpu.VMEM((n_row, p_size, width), BF16)],
            name="forward",
            work=1,
        )
        give_core, *near = lax.optimization_barrier((give_core, *near))
        came = over(give_core, "col", 1)
        near_own = jnp.stack([rounded, *near])
        near_far = over(near_own, "col", 1)
        keep, grams = call(
            gram_kernel,
            [shape((n_chip, p_size, width), F32), square],
            [acc_row, came, grams, rounded, *near],
            name="gram",
        )
        grams_came = over(grams, "col", 1)
        grams, *give = call(
            join_kernel, [square] + [message] * (n_chip - 1), [keep, grams, grams_came], name="join"
        )
        parts = [over(block, "col", 2 * d + 2) for d, block in enumerate(give)]
        (acc_col,) = call(
            mirrored_kernel,
            [shape((n_row, p_size, width), F32)],
            [index, near_own, near_far, held],
            [SMEM] + [VMEM] * 3,
            [pltpu.VMEM((n_col, p_size, width), BF16)],
            name="mirrored",
            work=passes,
        )
        mine, grams, *give = call(
            functools.partial(rows_kernel, n_in=n_chip - 1),
            [block32, square] + [message] * (n_row - 1),
            [keep, grams, own, acc_col, *parts],
            name="rows",
        )
        return mine, grams, [over(block, "row", d + 1) for d, block in enumerate(give)]

    small = shape((p_size, p_size), F32)
    (rounded,) = call(round_kernel, [block16], [probes], name="round", work=START)
    mine, grams, parts = apply_operator(rounded, probes)
    image, residual, rounded, totals, alpha = call(
        functools.partial(first_kernel, n_in=n_row - 1),
        [block32, block32, block16, square, small],
        [mine, grams, probes, *parts],
        name="first_step",
    )
    inverse, middle, solved = call(
        between_kernel, [small, small, block32], [totals, alpha, probes], name="between"
    )
    mine, grams, parts = apply_operator(rounded, residual)
    solved, residual = call(
        functools.partial(last_kernel, n_in=n_row - 1),
        [block32, block32],
        [mine, grams, probes, image, residual, inverse, middle, solved, *parts],
        name="last_step",
    )
    return solved[None], residual[None]


def solution(mesh):
    placed = (
        P("row", "col", None, None, None),
        P(("row", "col"), None, None),
        P(("row", "col"), None, None),
        P("row", "col", None),
        P("row", "col", None),
        P("row", "col"),
    )
    return jax.shard_map(
        functools.partial(body, mesh.shape["row"], mesh.shape["col"]),
        mesh=mesh,
        in_specs=placed,
        out_specs=(P(("row", "col"), None, None), P(("row", "col"), None, None)),
        check_vma=False,
    )
```

```python
import functools

import jax
import jax.numpy as jnp
from jax import lax
from jax.experimental import pallas as pl
from jax.experimental.pallas import tpu as pltpu
from jax.sharding import PartitionSpec as P

START = 10**10
F32 = jnp.float32
BF16 = jnp.bfloat16
HI = lax.Precision.HIGHEST
NT = (((1,), (1,)), ((), ()))
NN = (((1,), (0,)), ((), ()))
TN = (((0,), (0,)), ((), ()))
ANY = pl.BlockSpec(memory_space=pl.ANY)
VMEM = pl.BlockSpec(memory_space=pltpu.VMEM)
SMEM = pl.BlockSpec(memory_space=pltpu.SMEM)


def dot32(left, right, dims):
    return lax.dot_general(left, right, dims, precision=HI, preferred_element_type=F32)


def dot16(left, right, dims):
    return lax.dot_general(left, right, dims, preferred_element_type=F32)


def split16(value):
    first = value.astype(BF16)
    return first, (value - first.astype(F32)).astype(BF16)


def dot_exact16(left, right, dims):
    first, second = split16(right)
    return dot16(left, first, dims) + dot16(left, second, dims)


def dot_two(left, right, dims):
    first, second = split16(left)
    top, rest = split16(right)
    return dot16(first, top, dims) + (dot16(first, rest, dims) + dot16(second, top, dims))


def eliminate(systems, group=16):
    size, width = systems[0].shape
    rows = lax.broadcasted_iota(jnp.int32, (size, width), 0)
    scales = [jnp.zeros((size, width), F32) for system in systems]
    for start in range(0, size, group):
        for at, system in enumerate(systems):
            columns = [
                jnp.broadcast_to(system[:, k : k + 1], (size, width)) for k in range(start, start + group)
            ]
            for place, k in enumerate(range(start, start + group)):
                inverse = 1.0 / columns[place][k : k + 1, :]
                here = rows == k
                factors = jnp.where(here, 0.0, columns[place])
                scales[at] = jnp.where(here, inverse, scales[at])
                for later in range(place + 1, group):
                    columns[later] = columns[later] - factors * (columns[later][k : k + 1, :] * inverse)
                system = system - factors * (system[k : k + 1, :] * inverse)
            systems[at] = system
    return [(system * scale)[:, size:] for system, scale in zip(systems, scales)]


def compact(block):
    size, width = block.shape
    whole = width - width % 128
    rows = [block[:, at : at + 128] for at in range(0, whole, 128)]
    if whole < width:
        each = size * (width - whole) // 128
        tail = [block[at : at + each, whole:] for at in range(0, size, each)]
        rows.append(jnp.concatenate(tail, 1))
    return jnp.concatenate(rows, 0)


def spread(rows, size):
    width = rows.shape[0] * 128 // size
    whole, rest = width // 128, width % 128
    columns = [rows[k * size : (k + 1) * size] for k in range(whole)]
    if rest:
        tail = rows[whole * size :]
        columns.append(jnp.concatenate([tail[:, at : at + rest] for at in range(0, 128, rest)], 0))
    return jnp.concatenate(columns, 1)


def pack(block, grams):
    size = grams.shape[0]
    rows = lax.broadcasted_iota(jnp.int32, (size, size), 0)
    columns = lax.broadcasted_iota(jnp.int32, (size, size), 1)
    both = jnp.where(rows >= columns, grams[:, :size], grams[:, size:])
    diagonal = jnp.sum(jnp.where(rows == columns, grams[:, size:], 0.0), axis=0, keepdims=True)
    parts = jnp.concatenate(split16(both), 1)
    last = jnp.concatenate(split16(jnp.broadcast_to(diagonal, (16, size))), 1)
    return jnp.concatenate([compact(block), parts, last], 0)


def unpack(messages, size):
    end = messages[0].shape[0]
    blocks, parts, last = (
        sum(message[rows].astype(F32) for message in messages)
        for rows in (slice(0, end - 16 - size), slice(end - 16 - size, end - 16), slice(end - 16, end))
    )
    both = parts[:, :size] + parts[:, size:]
    diagonal = (last[:, :size] + last[:, size:])[:1]
    rows = lax.broadcasted_iota(jnp.int32, (size, size), 0)
    columns = lax.broadcasted_iota(jnp.int32, (size, size), 1)
    turned = both.T
    first = jnp.where(rows >= columns, both, turned)
    second = jnp.where(rows < columns, both, turned)
    second = jnp.where(rows == columns, diagonal, second)
    return spread(blocks, size), jnp.concatenate([first, second], 1)


def held_slots(count, slots, work):
    group = 4 if slots % 4 == 0 else 1

    def turn(g, carry):
        for u in range(group):
            work(g * group + u, g * group + u < count)
        return carry

    lax.fori_loop(0, (count + group - 1) // group, turn, 0)


def places(rows_list, cols_list, n_chip):
    row, column = lax.axis_index("row"), lax.axis_index("col")

    def place(slot):
        apart = rows_list[slot] ^ column
        return (apart % 2) * n_chip + apart // 2, cols_list[slot] ^ row

    return place


def round_kernel(value, out):
    out[...] = compact(value[...].astype(BF16))


def forward_kernel(counts, rows_list, cols_list, tiles, *rest, n_row):
    far_in = rest[:n_row]
    give_core, acc, far = rest[n_row:]
    n_chip = give_core.shape[0]
    slots = tiles.shape[0]
    place = places(rows_list, cols_list, n_chip)
    for d, block in enumerate(far_in):
        far[d] = spread(block[...], far.shape[1])
    acc[...] = jnp.zeros_like(acc)

    def work(slot, held):
        i, j = place(slot)
        acc[i] += jnp.where(held, dot16(far[j], tiles[slot], NT), 0.0)

    held_slots(counts[0], slots, work)
    for d in range(n_chip):
        give_core[d] = acc[n_chip + d].astype(BF16)


def own_kernel(near, diag, residual, after, own_out, grams):
    size = residual.shape[0]
    block = spread(near[...], size)
    own = dot16(block, diag[...], NT)
    own_out[...] = own
    half = 0.5 * dot_exact16(block, own, NT)
    grams[:, :size] = half + half.T
    grams[:, size:] = dot_two(residual[...], residual[...], NT)


def gram_kernel(acc, came, grams_own, *rest):
    *near, keep, grams = rest
    size = grams.shape[0]
    half = jnp.zeros((size, size), F32)
    for d, block in enumerate(near):
        both = acc[d] + came[d].astype(F32)
        keep[d] = both
        half += dot_exact16(spread(block[...], size), both, NT)
    grams[:, :size] = grams_own[:, :size] + half + half.T
    grams[:, size:] = grams_own[:, size:]


def mirrored_kernel(counts, rows_list, cols_list, near_own, near_far, tiles, acc, near):
    n_chip = near_own.shape[0]
    slots = tiles.shape[0]
    place = places(rows_list, cols_list, n_chip)
    for d in range(n_chip):
        near[d] = spread(near_own[d], near.shape[1])
        near[n_chip + d] = spread(near_far[d], near.shape[1])
    acc[...] = jnp.zeros_like(acc)

    def work(slot, held):
        i, j = place(slot)
        acc[j] += jnp.where(held, dot16(near[i], tiles[slot], NN), 0.0)

    held_slots(counts[0], slots, work)


def join_kernel(keep, grams, grams_came, grams_out, *give):
    total = grams[...] + grams_came[...]
    grams_out[...] = total
    for d in range(1, keep.shape[0]):
        give[d - 1][...] = pack(keep[d].astype(BF16), total)


def rows_kernel(keep, grams, own, acc, *rest, n_in):
    image, total, (mine_out, grams_out, *give) = gather_sums(keep[0], grams[...], rest, n_in)
    mine_out[...] = image + own[...] + acc[0]
    grams_out[...] = total
    for d in range(1, acc.shape[0]):
        give[d - 1][...] = pack(acc[d].astype(BF16), total)


def gather_sums(mine, grams, rest, n_in):
    block, matrices = unpack([message[...] for message in rest[:n_in]], mine.shape[0])
    return mine + block, grams + matrices, rest[n_in:]


def first_kernel(mine, grams, probes, *rest, n_in):
    image, total, (image_out, residual_out, rounded, totals, alpha_out) = gather_sums(
        mine[...], grams[...], rest, n_in
    )
    (alpha,) = eliminate([total])
    residual = probes[...] - dot_two(alpha, image, TN)
    rounded[...] = compact(residual.astype(BF16))
    residual_out[...] = residual
    image_out[...] = image
    totals[...] = total
    alpha_out[...] = alpha


def between_kernel(totals, alpha, probes, inverse_out, middle_out, solved_out):
    size = alpha.shape[0]
    eye = (
        lax.broadcasted_iota(jnp.int32, (size, size), 0)
        == lax.broadcasted_iota(jnp.int32, (size, size), 1)
    ).astype(F32)
    (inverse,) = eliminate([jnp.concatenate([totals[:, size:], eye], 1)])
    inverse_out[...] = inverse
    middle_out[...] = dot32(inverse, dot32(totals[:, :size], inverse, NN), TN)
    solved_out[...] = dot_two(alpha[...], probes[...], TN)


def last_kernel(mine, grams, probes, image_in, residual_in, inverse, middle, solved, *rest, n_in):
    forward, total, (solution_out, residual_out) = gather_sums(mine[...], grams[...], rest, n_in)
    size = forward.shape[0]
    norm = total[:, size:]
    curv = total[:, :size] - dot32(norm, dot32(middle[...], norm, NN), TN)
    beta = dot32(inverse[...], norm, NN)
    residual = residual_in[...]
    direction = residual + dot_two(beta, probes[...], TN)
    image = forward + dot_two(beta, image_in[...], TN)
    (step,) = eliminate([jnp.concatenate([curv, norm], 1)])
    solution_out[...] = solved[...] + dot_two(step, direction, TN)
    residual_out[...] = residual - dot_two(step, image, TN)


def call(kernel, outs, args, specs=None, scratch=(), limit=32, name=None, work=None):
    return pl.pallas_call(
        kernel,
        out_shape=outs,
        in_specs=[VMEM] * len(args) if specs is None else specs,
        out_specs=[VMEM] * len(outs),
        scratch_shapes=list(scratch),
        compiler_params=pltpu.CompilerParams(vmem_limit_bytes=limit << 20),
        cost_estimate=None if work is None else pl.CostEstimate(flops=work, bytes_accessed=0, transcendentals=0),
        name=name,
    )(*args)


def body(n_row, n_col, tiles, diag_tiles, probes, rows_list, cols_list, counts):
    n_chip = n_col // 2
    p_size, width = probes.shape[1:]
    shape = jax.ShapeDtypeStruct
    block32 = shape((p_size, width), F32)
    block16 = shape((p_size * width // 128, 128), BF16)

    def over(value, axis, delta):
        size = n_row if axis == "row" else n_col
        return lax.ppermute(value, axis, [(i, i ^ delta) for i in range(size)])

    def over_chips(value):
        return [over(value, "col", 2 * d) for d in range(1, n_chip)]

    def over_rows(value):
        return [over(value, "row", d) for d in range(1, n_row)]

    index = [counts[0], rows_list[0, 0], cols_list[0, 0]]
    probes = probes[0]
    diag = diag_tiles[0]
    held = tiles[0, 0]
    square = shape((p_size, 2 * p_size), F32)
    slots = tiles.shape[2]
    passes = 2 * slots * p_size * width * width

    message = shape((block16.shape[0] + p_size + 16, 128), BF16)

    def apply_operator(rounded, residual):
        from_rows = over_rows(rounded)
        near = over_chips(rounded)
        give_core, acc_row = call(
            functools.partial(forward_kernel, n_row=n_row),
            [shape((n_chip, p_size, width), BF16), shape((n_col, p_size, width), F32)],
            [*index, held, rounded, *from_rows],
            [SMEM] * 3 + [VMEM] * (1 + n_row),
            [pltpu.VMEM((n_row, p_size, width), BF16)],
            name="forward",
            work=1,
        )
        give_core, *near = lax.optimization_barrier((give_core, *near))
        came = over(give_core, "col", 1)
        own, grams = call(
            own_kernel, [block32, square], [rounded, diag, residual, acc_row], [VMEM] * 3 + [ANY], name="own"
        )
        near_own = jnp.stack([rounded, *near])
        near_far = over(near_own, "col", 1)
        keep, grams = call(
            gram_kernel,
            [shape((n_chip, p_size, width), F32), square],
            [acc_row, came, grams, rounded, *near],
            name="gram",
        )
        grams_came = over(grams, "col", 1)
        grams, *give = call(
            join_kernel, [square] + [message] * (n_chip - 1), [keep, grams, grams_came], name="join"
        )
        parts = [over(block, "col", 2 * d + 2) for d, block in enumerate(give)]
        (acc_col,) = call(
            mirrored_kernel,
            [shape((n_row, p_size, width), F32)],
            [*index, near_own, near_far, held],
            [SMEM] * 3 + [VMEM] * 3,
            [pltpu.VMEM((n_col, p_size, width), BF16)],
            name="mirrored",
            work=passes,
        )
        mine, grams, *give = call(
            functools.partial(rows_kernel, n_in=n_chip - 1),
            [block32, square] + [message] * (n_row - 1),
            [keep, grams, own, acc_col, *parts],
            name="rows",
        )
        return mine, grams, [over(block, "row", d + 1) for d, block in enumerate(give)]

    small = shape((p_size, p_size), F32)
    (rounded,) = call(round_kernel, [block16], [probes], name="round", work=START)
    mine, grams, parts = apply_operator(rounded, probes)
    image, residual, rounded, totals, alpha = call(
        functools.partial(first_kernel, n_in=n_row - 1),
        [block32, block32, block16, square, small],
        [mine, grams, probes, *parts],
        name="first_step",
    )
    inverse, middle, solved = call(
        between_kernel, [small, small, block32], [totals, alpha, probes], name="between"
    )
    mine, grams, parts = apply_operator(rounded, residual)
    solved, residual = call(
        functools.partial(last_kernel, n_in=n_row - 1),
        [block32, block32],
        [mine, grams, probes, image, residual, inverse, middle, solved, *parts],
        name="last_step",
    )
    return solved[None], residual[None]


def solution(mesh):
    placed = (
        P("row", "col", None, None, None),
        P(("row", "col"), None, None),
        P(("row", "col"), None, None),
        P("row", "col", None),
        P("row", "col", None),
        P("row", "col"),
    )
    return jax.shard_map(
        functools.partial(body, mesh.shape["row"], mesh.shape["col"]),
        mesh=mesh,
        in_specs=placed,
        out_specs=(P(("row", "col"), None, None), P(("row", "col"), None, None)),
        check_vma=False,
    )
```

```python
import functools

import jax
import jax.numpy as jnp
from jax import lax
from jax.experimental import pallas as pl
from jax.experimental.pallas import tpu as pltpu
from jax.sharding import PartitionSpec as P

START = 10**10
F32 = jnp.float32
BF16 = jnp.bfloat16
HI = lax.Precision.HIGHEST
NT = (((1,), (1,)), ((), ()))
NN = (((1,), (0,)), ((), ()))
TN = (((0,), (0,)), ((), ()))
ANY = pl.BlockSpec(memory_space=pl.ANY)
VMEM = pl.BlockSpec(memory_space=pltpu.VMEM)
SMEM = pl.BlockSpec(memory_space=pltpu.SMEM)


def dot32(left, right, dims):
    return lax.dot_general(left, right, dims, precision=HI, preferred_element_type=F32)


def dot16(left, right, dims):
    return lax.dot_general(left, right, dims, preferred_element_type=F32)


def split16(value):
    first = value.astype(BF16)
    return first, (value - first.astype(F32)).astype(BF16)


def dot_exact16(left, right, dims):
    first, second = split16(right)
    return dot16(left, first, dims) + dot16(left, second, dims)


def dot_two(left, right, dims):
    first, second = split16(left)
    top, rest = split16(right)
    return dot16(first, top, dims) + (dot16(first, rest, dims) + dot16(second, top, dims))


def eliminate(systems, group=16):
    size, width = systems[0].shape
    rows = lax.broadcasted_iota(jnp.int32, (size, width), 0)
    scales = [jnp.zeros((size, width), F32) for system in systems]
    for start in range(0, size, group):
        for at, system in enumerate(systems):
            columns = [
                jnp.broadcast_to(system[:, k : k + 1], (size, width)) for k in range(start, start + group)
            ]
            for place, k in enumerate(range(start, start + group)):
                inverse = 1.0 / columns[place][k : k + 1, :]
                here = rows == k
                factors = jnp.where(here, 0.0, columns[place])
                scales[at] = jnp.where(here, inverse, scales[at])
                for later in range(place + 1, group):
                    columns[later] = columns[later] - factors * (columns[later][k : k + 1, :] * inverse)
                system = system - factors * (system[k : k + 1, :] * inverse)
            systems[at] = system
    return [(system * scale)[:, size:] for system, scale in zip(systems, scales)]


def compact(block):
    size, width = block.shape
    whole = width - width % 128
    rows = [block[:, at : at + 128] for at in range(0, whole, 128)]
    if whole < width:
        each = size * (width - whole) // 128
        tail = [block[at : at + each, whole:] for at in range(0, size, each)]
        rows.append(jnp.concatenate(tail, 1))
    return jnp.concatenate(rows, 0)


def spread(rows, size):
    width = rows.shape[0] * 128 // size
    whole, rest = width // 128, width % 128
    columns = [rows[k * size : (k + 1) * size] for k in range(whole)]
    if rest:
        tail = rows[whole * size :]
        columns.append(jnp.concatenate([tail[:, at : at + rest] for at in range(0, 128, rest)], 0))
    return jnp.concatenate(columns, 1)


def pack(block, grams):
    size = grams.shape[0]
    rows = lax.broadcasted_iota(jnp.int32, (size, size), 0)
    columns = lax.broadcasted_iota(jnp.int32, (size, size), 1)
    both = jnp.where(rows >= columns, grams[:, :size], grams[:, size:])
    diagonal = jnp.sum(jnp.where(rows == columns, grams[:, size:], 0.0), axis=0, keepdims=True)
    parts = jnp.concatenate(split16(both), 1)
    last = jnp.concatenate(split16(jnp.broadcast_to(diagonal, (16, size))), 1)
    return jnp.concatenate([compact(block), parts, last], 0)


def unpack(messages, size):
    end = messages[0].shape[0]
    blocks, parts, last = (
        sum(message[rows].astype(F32) for message in messages)
        for rows in (slice(0, end - 16 - size), slice(end - 16 - size, end - 16), slice(end - 16, end))
    )
    both = parts[:, :size] + parts[:, size:]
    diagonal = (last[:, :size] + last[:, size:])[:1]
    rows = lax.broadcasted_iota(jnp.int32, (size, size), 0)
    columns = lax.broadcasted_iota(jnp.int32, (size, size), 1)
    turned = both.T
    first = jnp.where(rows >= columns, both, turned)
    second = jnp.where(rows < columns, both, turned)
    second = jnp.where(rows == columns, diagonal, second)
    return spread(blocks, size), jnp.concatenate([first, second], 1)


def held_slots(count, slots, work):
    group = 4 if slots % 4 == 0 else 1

    def turn(g, carry):
        for u in range(group):
            work(g * group + u, g * group + u < count)
        return carry

    lax.fori_loop(0, (count + group - 1) // group, turn, 0)


def places(rows_list, cols_list, n_chip):
    row, column = lax.axis_index("row"), lax.axis_index("col")

    def place(slot):
        apart = rows_list[slot] ^ column
        return (apart % 2) * n_chip + apart // 2, cols_list[slot] ^ row

    return place


def round_kernel(value, out):
    out[...] = compact(value[...].astype(BF16))


def turn_kernel(counts, tiles, after, out):
    def work(slot, held):
        out[slot] = tiles[slot].T

    held_slots(counts[0], tiles.shape[0], work)


def forward_kernel(counts, rows_list, cols_list, tiles, *rest, n_row, dims):
    far_in = rest[:n_row]
    give_core, acc, far = rest[n_row:]
    n_chip = give_core.shape[0]
    slots = tiles.shape[0]
    place = places(rows_list, cols_list, n_chip)
    for d, block in enumerate(far_in):
        far[d] = spread(block[...], far.shape[1])
    acc[...] = jnp.zeros_like(acc)

    def work(slot, held):
        i, j = place(slot)
        acc[i] += jnp.where(held, dot16(far[j], tiles[slot], dims), 0.0)

    held_slots(counts[0], slots, work)
    for d in range(n_chip):
        give_core[d] = acc[n_chip + d].astype(BF16)


def own_kernel(near, diag, residual, after, own_out, grams):
    size = residual.shape[0]
    block = spread(near[...], size)
    own = dot16(block, diag[...], NT)
    own_out[...] = own
    half = 0.5 * dot_exact16(block, own, NT)
    grams[:, :size] = half + half.T
    grams[:, size:] = dot_two(residual[...], residual[...], NT)


def gram_kernel(acc, came, grams_own, *rest):
    *near, keep, grams = rest
    size = grams.shape[0]
    half = jnp.zeros((size, size), F32)
    for d, block in enumerate(near):
        both = acc[d] + came[d].astype(F32)
        keep[d] = both
        half += dot_exact16(spread(block[...], size), both, NT)
    grams[:, :size] = grams_own[:, :size] + half + half.T
    grams[:, size:] = grams_own[:, size:]


def mirrored_kernel(counts, rows_list, cols_list, near_own, near_far, tiles, acc, near):
    n_chip = near_own.shape[0]
    slots = tiles.shape[0]
    place = places(rows_list, cols_list, n_chip)
    for d in range(n_chip):
        near[d] = spread(near_own[d], near.shape[1])
        near[n_chip + d] = spread(near_far[d], near.shape[1])
    acc[...] = jnp.zeros_like(acc)

    def work(slot, held):
        i, j = place(slot)
        acc[j] += jnp.where(held, dot16(near[i], tiles[slot], NN), 0.0)

    held_slots(counts[0], slots, work)


def join_kernel(keep, grams, grams_came, grams_out, *give):
    total = grams[...] + grams_came[...]
    grams_out[...] = total
    for d in range(1, keep.shape[0]):
        give[d - 1][...] = pack(keep[d].astype(BF16), total)


def rows_kernel(keep, grams, own, acc, *rest, n_in):
    image, total, (mine_out, grams_out, *give) = gather_sums(keep[0], grams[...], rest, n_in)
    mine_out[...] = image + own[...] + acc[0]
    grams_out[...] = total
    for d in range(1, acc.shape[0]):
        give[d - 1][...] = pack(acc[d].astype(BF16), total)


def gather_sums(mine, grams, rest, n_in):
    block, matrices = unpack([message[...] for message in rest[:n_in]], mine.shape[0])
    return mine + block, grams + matrices, rest[n_in:]


def first_kernel(mine, grams, probes, *rest, n_in):
    image, total, (image_out, residual_out, rounded, totals, alpha_out) = gather_sums(
        mine[...], grams[...], rest, n_in
    )
    (alpha,) = eliminate([total])
    residual = probes[...] - dot_two(alpha, image, TN)
    rounded[...] = compact(residual.astype(BF16))
    residual_out[...] = residual
    image_out[...] = image
    totals[...] = total
    alpha_out[...] = alpha


def between_kernel(totals, alpha, probes, inverse_out, middle_out, solved_out):
    size = alpha.shape[0]
    eye = (
        lax.broadcasted_iota(jnp.int32, (size, size), 0)
        == lax.broadcasted_iota(jnp.int32, (size, size), 1)
    ).astype(F32)
    (inverse,) = eliminate([jnp.concatenate([totals[:, size:], eye], 1)])
    inverse_out[...] = inverse
    middle_out[...] = dot32(inverse, dot32(totals[:, :size], inverse, NN), TN)
    solved_out[...] = dot_two(alpha[...], probes[...], TN)


def last_kernel(mine, grams, probes, image_in, residual_in, inverse, middle, solved, *rest, n_in):
    forward, total, (solution_out, residual_out) = gather_sums(mine[...], grams[...], rest, n_in)
    size = forward.shape[0]
    norm = total[:, size:]
    curv = total[:, :size] - dot32(norm, dot32(middle[...], norm, NN), TN)
    beta = dot32(inverse[...], norm, NN)
    residual = residual_in[...]
    direction = residual + dot_two(beta, probes[...], TN)
    image = forward + dot_two(beta, image_in[...], TN)
    (step,) = eliminate([jnp.concatenate([curv, norm], 1)])
    solution_out[...] = solved[...] + dot_two(step, direction, TN)
    residual_out[...] = residual - dot_two(step, image, TN)


def call(kernel, outs, args, specs=None, scratch=(), limit=24, name=None, work=None):
    return pl.pallas_call(
        kernel,
        out_shape=outs,
        in_specs=[VMEM] * len(args) if specs is None else specs,
        out_specs=[VMEM] * len(outs),
        scratch_shapes=list(scratch),
        compiler_params=pltpu.CompilerParams(vmem_limit_bytes=limit << 20),
        cost_estimate=None if work is None else pl.CostEstimate(flops=work, bytes_accessed=0, transcendentals=0),
        name=name,
    )(*args)


def body(n_row, n_col, tiles, diag_tiles, probes, rows_list, cols_list, counts):
    n_chip = n_col // 2
    p_size, width = probes.shape[1:]
    shape = jax.ShapeDtypeStruct
    block32 = shape((p_size, width), F32)
    block16 = shape((p_size * width // 128, 128), BF16)

    def over(value, axis, delta):
        size = n_row if axis == "row" else n_col
        return lax.ppermute(value, axis, [(i, i ^ delta) for i in range(size)])

    def over_chips(value):
        return [over(value, "col", 2 * d) for d in range(1, n_chip)]

    def over_rows(value):
        return [over(value, "row", d) for d in range(1, n_row)]

    index = [counts[0], rows_list[0, 0], cols_list[0, 0]]
    probes = probes[0]
    diag = diag_tiles[0]
    held = tiles[0, 0]
    square = shape((p_size, 2 * p_size), F32)
    slots = tiles.shape[2]
    passes = 2 * slots * p_size * width * width

    message = shape((block16.shape[0] + p_size + 16, 128), BF16)

    def apply_operator(rounded, residual, turned=None):
        from_rows = over_rows(rounded)
        near = over_chips(rounded)
        give_core, acc_row = call(
            functools.partial(forward_kernel, n_row=n_row, dims=NT if turned is None else NN),
            [shape((n_chip, p_size, width), BF16), shape((n_col, p_size, width), F32)],
            [*index, held if turned is None else turned, rounded, *from_rows],
            [SMEM] * 3 + [VMEM] * (1 + n_row),
            [pltpu.VMEM((n_row, p_size, width), BF16)],
            name="forward",
            work=1,
        )
        give_core, *near = lax.optimization_barrier((give_core, *near))
        came = over(give_core, "col", 1)
        own, grams = call(
            own_kernel, [block32, square], [rounded, diag, residual, acc_row], [VMEM] * 3 + [ANY], name="own"
        )
        near_own = jnp.stack([rounded, *near])
        near_far = over(near_own, "col", 1)
        keep, grams = call(
            gram_kernel,
            [shape((n_chip, p_size, width), F32), square],
            [acc_row, came, grams, rounded, *near],
            name="gram",
        )
        grams_came = over(grams, "col", 1)
        grams, *give = call(
            join_kernel, [square] + [message] * (n_chip - 1), [keep, grams, grams_came], name="join"
        )
        parts = [over(block, "col", 2 * d + 2) for d, block in enumerate(give)]
        (acc_col,) = call(
            mirrored_kernel,
            [shape((n_row, p_size, width), F32)],
            [*index, near_own, near_far, held],
            [SMEM] * 3 + [VMEM] * 3,
            [pltpu.VMEM((n_col, p_size, width), BF16)],
            name="mirrored",
            work=passes,
        )
        mine, grams, *give = call(
            functools.partial(rows_kernel, n_in=n_chip - 1),
            [block32, square] + [message] * (n_row - 1),
            [keep, grams, own, acc_col, *parts],
            name="rows",
        )
        parts = [over(block, "row", d + 1) for d, block in enumerate(give)]
        if turned is None:
            (turned,) = call(
                turn_kernel,
                [shape(held.shape, BF16)],
                [index[0], held, grams],
                [SMEM, VMEM, ANY],
                name="turn",
                limit=28,
            )
            turned, *parts = lax.optimization_barrier((turned, *parts))
        return mine, grams, parts, turned

    small = shape((p_size, p_size), F32)
    (rounded,) = call(round_kernel, [block16], [probes], name="round", work=START)
    mine, grams, parts, turned = apply_operator(rounded, probes)
    image, residual, rounded, totals, alpha = call(
        functools.partial(first_kernel, n_in=n_row - 1),
        [block32, block32, block16, square, small],
        [mine, grams, probes, *parts],
        name="first_step",
    )
    inverse, middle, solved = call(
        between_kernel, [small, small, block32], [totals, alpha, probes], name="between"
    )
    mine, grams, parts, turned = apply_operator(rounded, residual, turned)
    solved, residual = call(
        functools.partial(last_kernel, n_in=n_row - 1),
        [block32, block32],
        [mine, grams, probes, image, residual, inverse, middle, solved, *parts],
        name="last_step",
    )
    return solved[None], residual[None]


def solution(mesh):
    placed = (
        P("row", "col", None, None, None),
        P(("row", "col"), None, None),
        P(("row", "col"), None, None),
        P("row", "col", None),
        P("row", "col", None),
        P("row", "col"),
    )
    return jax.shard_map(
        functools.partial(body, mesh.shape["row"], mesh.shape["col"]),
        mesh=mesh,
        in_specs=placed,
        out_specs=(P(("row", "col"), None, None), P(("row", "col"), None, None)),
        check_vma=False,
    )
```

```python
import functools

import jax
import jax.numpy as jnp
from jax import lax
from jax.experimental import pallas as pl
from jax.experimental.pallas import tpu as pltpu
from jax.sharding import PartitionSpec as P

START = 10**10
F32 = jnp.float32
BF16 = jnp.bfloat16
HI = lax.Precision.HIGHEST
NT = (((1,), (1,)), ((), ()))
NN = (((1,), (0,)), ((), ()))
TN = (((0,), (0,)), ((), ()))
ANY = pl.BlockSpec(memory_space=pl.ANY)
VMEM = pl.BlockSpec(memory_space=pltpu.VMEM)
SMEM = pl.BlockSpec(memory_space=pltpu.SMEM)


def dot32(left, right, dims):
    return lax.dot_general(left, right, dims, precision=HI, preferred_element_type=F32)


def dot16(left, right, dims):
    return lax.dot_general(left, right, dims, preferred_element_type=F32)


def split16(value):
    first = value.astype(BF16)
    return first, (value - first.astype(F32)).astype(BF16)


def dot_exact16(left, right, dims):
    first, second = split16(right)
    return dot16(left, first, dims) + dot16(left, second, dims)


def dot_two(left, right, dims):
    first, second = split16(left)
    top, rest = split16(right)
    return dot16(first, top, dims) + (dot16(first, rest, dims) + dot16(second, top, dims))


def eliminate(systems, group=16):
    size, width = systems[0].shape
    rows = lax.broadcasted_iota(jnp.int32, (size, width), 0)
    scales = [jnp.zeros((size, width), F32) for system in systems]
    for start in range(0, size, group):
        for at, system in enumerate(systems):
            columns = [
                jnp.broadcast_to(system[:, k : k + 1], (size, width)) for k in range(start, start + group)
            ]
            for place, k in enumerate(range(start, start + group)):
                inverse = 1.0 / columns[place][k : k + 1, :]
                here = rows == k
                factors = jnp.where(here, 0.0, columns[place])
                scales[at] = jnp.where(here, inverse, scales[at])
                for later in range(place + 1, group):
                    columns[later] = columns[later] - factors * (columns[later][k : k + 1, :] * inverse)
                system = system - factors * (system[k : k + 1, :] * inverse)
            systems[at] = system
    return [(system * scale)[:, size:] for system, scale in zip(systems, scales)]


def compact(block):
    size, width = block.shape
    whole = width - width % 128
    rows = [block[:, at : at + 128] for at in range(0, whole, 128)]
    if whole < width:
        each = size * (width - whole) // 128
        tail = [block[at : at + each, whole:] for at in range(0, size, each)]
        rows.append(jnp.concatenate(tail, 1))
    return jnp.concatenate(rows, 0)


def spread(rows, size):
    width = rows.shape[0] * 128 // size
    whole, rest = width // 128, width % 128
    columns = [rows[k * size : (k + 1) * size] for k in range(whole)]
    if rest:
        tail = rows[whole * size :]
        columns.append(jnp.concatenate([tail[:, at : at + rest] for at in range(0, 128, rest)], 0))
    return jnp.concatenate(columns, 1)


def pack(block, grams):
    size = grams.shape[0]
    rows = lax.broadcasted_iota(jnp.int32, (size, size), 0)
    columns = lax.broadcasted_iota(jnp.int32, (size, size), 1)
    both = jnp.where(rows >= columns, grams[:, :size], grams[:, size:])
    diagonal = jnp.sum(jnp.where(rows == columns, grams[:, size:], 0.0), axis=0, keepdims=True)
    parts = jnp.concatenate(split16(both), 1)
    last = jnp.concatenate(split16(jnp.broadcast_to(diagonal, (16, size))), 1)
    return jnp.concatenate([compact(block), parts, last], 0)


def unpack(messages, size):
    end = messages[0].shape[0]
    blocks, parts, last = (
        sum(message[rows].astype(F32) for message in messages)
        for rows in (slice(0, end - 16 - size), slice(end - 16 - size, end - 16), slice(end - 16, end))
    )
    both = parts[:, :size] + parts[:, size:]
    diagonal = (last[:, :size] + last[:, size:])[:1]
    rows = lax.broadcasted_iota(jnp.int32, (size, size), 0)
    columns = lax.broadcasted_iota(jnp.int32, (size, size), 1)
    turned = both.T
    first = jnp.where(rows >= columns, both, turned)
    second = jnp.where(rows < columns, both, turned)
    second = jnp.where(rows == columns, diagonal, second)
    return spread(blocks, size), jnp.concatenate([first, second], 1)


def held_slots(count, slots, work):
    group = 4 if slots % 4 == 0 else 1

    def turn(g, carry):
        for u in range(group):
            work(g * group + u, g * group + u < count)
        return carry

    lax.fori_loop(0, (count + group - 1) // group, turn, 0)


def places(rows_list, cols_list, n_chip):
    row, column = lax.axis_index("row"), lax.axis_index("col")

    def place(slot):
        apart = rows_list[slot] ^ column
        return (apart % 2) * n_chip + apart // 2, cols_list[slot] ^ row

    return place


def round_kernel(value, out):
    out[...] = compact(value[...].astype(BF16))


def turn_kernel(counts, tiles, after, out):
    def work(slot, held):
        out[slot] = tiles[slot].T

    held_slots(counts[0], tiles.shape[0], work)


def forward_kernel(counts, rows_list, cols_list, tiles, after, *rest, n_row, dims):
    far_in = rest[:n_row]
    give_core, acc, far = rest[n_row:]
    n_chip = give_core.shape[0]
    slots = tiles.shape[0]
    place = places(rows_list, cols_list, n_chip)
    for d, block in enumerate(far_in):
        far[d] = spread(block[...], far.shape[1])
    acc[...] = jnp.zeros_like(acc)

    def work(slot, held):
        i, j = place(slot)
        acc[i] += jnp.where(held, dot16(far[j], tiles[slot], dims), 0.0)

    held_slots(counts[0], slots, work)
    for d in range(n_chip):
        give_core[d] = acc[n_chip + d].astype(BF16)


def own_kernel(near, diag, residual, own_out, grams):
    size = residual.shape[0]
    block = spread(near[...], size)
    own = dot16(block, diag[...], NT)
    own_out[...] = own
    half = 0.5 * dot_exact16(block, own, NT)
    grams[:, :size] = half + half.T
    grams[:, size:] = dot_two(residual[...], residual[...], NT)


def near_kernel(acc, grams_own, *rest):
    *near, grams = rest
    size = grams.shape[0]
    half = jnp.zeros((size, size), F32)
    for d, block in enumerate(near):
        half += dot_exact16(spread(block[...], size), acc[d], NT)
    grams[:, :size] = grams_own[:, :size] + half + half.T
    grams[:, size:] = grams_own[:, size:]


def gram_kernel(came, grams_in, *rest):
    *near, grams = rest
    size = grams.shape[0]
    half = jnp.zeros((size, size), F32)
    for d, block in enumerate(near):
        half += dot16(spread(block[...], size), came[d], NT)
    grams[:, :size] = grams_in[:, :size] + half + half.T
    grams[:, size:] = grams_in[:, size:]


def mirrored_kernel(counts, rows_list, cols_list, near_own, near_far, tiles, acc, near):
    n_chip = near_own.shape[0]
    slots = tiles.shape[0]
    place = places(rows_list, cols_list, n_chip)
    for d in range(n_chip):
        near[d] = spread(near_own[d], near.shape[1])
        near[n_chip + d] = spread(near_far[d], near.shape[1])
    acc[...] = jnp.zeros_like(acc)

    def work(slot, held):
        i, j = place(slot)
        acc[j] += jnp.where(held, dot16(near[i], tiles[slot], NN), 0.0)

    held_slots(counts[0], slots, work)


def join_kernel(acc, came, grams, grams_came, mine, grams_out, *give):
    mine[...] = acc[0] + came[0].astype(F32)
    total = grams[...] + grams_came[...]
    grams_out[...] = total
    for d in range(1, came.shape[0]):
        give[d - 1][...] = pack((acc[d] + came[d].astype(F32)).astype(BF16), total)


def rows_kernel(mine, grams, own, acc, *rest, n_in):
    image, total, (mine_out, grams_out, *give) = gather_sums(mine[...], grams[...], rest, n_in)
    mine_out[...] = image + own[...] + acc[0]
    grams_out[...] = total
    for d in range(1, acc.shape[0]):
        give[d - 1][...] = pack(acc[d].astype(BF16), total)


def gather_sums(mine, grams, rest, n_in):
    block, matrices = unpack([message[...] for message in rest[:n_in]], mine.shape[0])
    return mine + block, grams + matrices, rest[n_in:]


def first_kernel(mine, grams, probes, *rest, n_in):
    image, total, (image_out, residual_out, rounded, totals, alpha_out) = gather_sums(
        mine[...], grams[...], rest, n_in
    )
    (alpha,) = eliminate([total])
    residual = probes[...] - dot_two(alpha, image, TN)
    rounded[...] = compact(residual.astype(BF16))
    residual_out[...] = residual
    image_out[...] = image
    totals[...] = total
    alpha_out[...] = alpha


def between_kernel(totals, alpha, probes, inverse_out, middle_out, solved_out):
    size = alpha.shape[0]
    eye = (
        lax.broadcasted_iota(jnp.int32, (size, size), 0)
        == lax.broadcasted_iota(jnp.int32, (size, size), 1)
    ).astype(F32)
    (inverse,) = eliminate([jnp.concatenate([totals[:, size:], eye], 1)])
    inverse_out[...] = inverse
    middle_out[...] = dot32(inverse, dot32(totals[:, :size], inverse, NN), TN)
    solved_out[...] = dot_two(alpha[...], probes[...], TN)


def last_kernel(mine, grams, probes, image_in, residual_in, inverse, middle, solved, *rest, n_in):
    forward, total, (solution_out, residual_out) = gather_sums(mine[...], grams[...], rest, n_in)
    size = forward.shape[0]
    norm = total[:, size:]
    curv = total[:, :size] - dot_two(norm, dot_two(middle[...], norm, NN), TN)
    beta = dot_two(inverse[...], norm, NN)
    residual = residual_in[...]
    direction = residual + dot_two(beta, probes[...], TN)
    image = forward + dot_two(beta, image_in[...], TN)
    (step,) = eliminate([jnp.concatenate([curv, norm], 1)])
    solution_out[...] = solved[...] + dot_two(step, direction, TN)
    residual_out[...] = residual - dot_two(step, image, TN)


def call(kernel, outs, args, specs=None, scratch=(), limit=24, name=None, work=None):
    return pl.pallas_call(
        kernel,
        out_shape=outs,
        in_specs=[VMEM] * len(args) if specs is None else specs,
        out_specs=[VMEM] * len(outs),
        scratch_shapes=list(scratch),
        compiler_params=pltpu.CompilerParams(vmem_limit_bytes=limit << 20),
        cost_estimate=None if work is None else pl.CostEstimate(flops=work, bytes_accessed=0, transcendentals=0),
        name=name,
    )(*args)


def body(n_row, n_col, tiles, diag_tiles, probes, rows_list, cols_list, counts):
    n_chip = n_col // 2
    p_size, width = probes.shape[1:]
    shape = jax.ShapeDtypeStruct
    block32 = shape((p_size, width), F32)
    block16 = shape((p_size * width // 128, 128), BF16)

    def over(value, axis, delta):
        size = n_row if axis == "row" else n_col
        return lax.ppermute(value, axis, [(i, i ^ delta) for i in range(size)])

    def over_chips(value):
        return [over(value, "col", 2 * d) for d in range(1, n_chip)]

    def over_rows(value):
        return [over(value, "row", d) for d in range(1, n_row)]

    index = [counts[0], rows_list[0, 0], cols_list[0, 0]]
    probes = probes[0]
    diag = diag_tiles[0]
    held = tiles[0, 0]
    square = shape((p_size, 2 * p_size), F32)
    slots = tiles.shape[2]
    passes = 2 * slots * p_size * width * width

    message = shape((block16.shape[0] + p_size + 16, 128), BF16)

    def apply_operator(rounded, residual, turned=None):
        from_rows = over_rows(rounded)
        near = over_chips(rounded)
        own, grams = call(own_kernel, [block32, square], [rounded, diag, residual], name="own")
        give_core, acc_row = call(
            functools.partial(forward_kernel, n_row=n_row, dims=NT if turned is None else NN),
            [shape((n_chip, p_size, width), BF16), shape((n_col, p_size, width), F32)],
            [*index, held if turned is None else turned, grams, rounded, *from_rows],
            [SMEM] * 3 + [VMEM, ANY] + [VMEM] * n_row,
            [pltpu.VMEM((n_row, p_size, width), BF16)],
            name="forward",
            work=1,
        )
        give_core, *near = lax.optimization_barrier((give_core, *near))
        came = over(give_core, "col", 1)
        near_own = jnp.stack([rounded, *near])
        near_far = over(near_own, "col", 1)
        (grams,) = call(near_kernel, [square], [acc_row, grams, rounded, *near], name="near")
        (grams,) = call(gram_kernel, [square], [came, grams, rounded, *near], name="gram")
        grams_came = over(grams, "col", 1)
        mine, grams, *give = call(
            join_kernel, [block32, square] + [message] * (n_chip - 1), [acc_row, came, grams, grams_came], name="join"
        )
        parts = [over(block, "col", 2 * d + 2) for d, block in enumerate(give)]
        (acc_col,) = call(
            mirrored_kernel,
            [shape((n_row, p_size, width), F32)],
            [*index, near_own, near_far, held],
            [SMEM] * 3 + [VMEM] * 3,
            [pltpu.VMEM((n_col, p_size, width), BF16)],
            name="mirrored",
            work=passes,
        )
        mine, grams, *give = call(
            functools.partial(rows_kernel, n_in=n_chip - 1),
            [block32, square] + [message] * (n_row - 1),
            [mine, grams, own, acc_col, *parts],
            name="rows",
        )
        parts = [over(block, "row", d + 1) for d, block in enumerate(give)]
        if turned is None:
            (turned,) = call(
                turn_kernel,
                [shape(held.shape, BF16)],
                [index[0], held, grams],
                [SMEM, VMEM, ANY],
                name="turn",
                limit=28,
            )
            turned, *parts = lax.optimization_barrier((turned, *parts))
        return mine, grams, parts, turned

    small = shape((p_size, p_size), F32)
    (rounded,) = call(round_kernel, [block16], [probes], name="round", work=START)
    mine, grams, parts, turned = apply_operator(rounded, probes)
    image, residual, rounded, totals, alpha = call(
        functools.partial(first_kernel, n_in=n_row - 1),
        [block32, block32, block16, square, small],
        [mine, grams, probes, *parts],
        name="first_step",
    )
    inverse, middle, solved = call(
        between_kernel, [small, small, block32], [totals, alpha, probes], name="between"
    )
    mine, grams, parts, turned = apply_operator(rounded, residual, turned)
    solved, residual = call(
        functools.partial(last_kernel, n_in=n_row - 1),
        [block32, block32],
        [mine, grams, probes, image, residual, inverse, middle, solved, *parts],
        name="last_step",
    )
    return solved[None], residual[None]


def solution(mesh):
    placed = (
        P("row", "col", None, None, None),
        P(("row", "col"), None, None),
        P(("row", "col"), None, None),
        P("row", "col", None),
        P("row", "col", None),
        P("row", "col"),
    )
    return jax.shard_map(
        functools.partial(body, mesh.shape["row"], mesh.shape["col"]),
        mesh=mesh,
        in_specs=placed,
        out_specs=(P(("row", "col"), None, None), P(("row", "col"), None, None)),
        check_vma=False,
    )
```

```python
import functools

import jax
import jax.numpy as jnp
from jax import lax
from jax.experimental import pallas as pl
from jax.experimental.pallas import tpu as pltpu
from jax.sharding import PartitionSpec as P

START = 10**10
F32 = jnp.float32
BF16 = jnp.bfloat16
HI = lax.Precision.HIGHEST
NT = (((1,), (1,)), ((), ()))
NN = (((1,), (0,)), ((), ()))
TN = (((0,), (0,)), ((), ()))
ANY = pl.BlockSpec(memory_space=pl.ANY)
VMEM = pl.BlockSpec(memory_space=pltpu.VMEM)
SMEM = pl.BlockSpec(memory_space=pltpu.SMEM)


def dot32(left, right, dims):
    return lax.dot_general(left, right, dims, precision=HI, preferred_element_type=F32)


def dot16(left, right, dims):
    return lax.dot_general(left, right, dims, preferred_element_type=F32)


def split16(value):
    first = value.astype(BF16)
    return first, (value - first.astype(F32)).astype(BF16)


def dot_exact16(left, right, dims):
    first, second = split16(right)
    return dot16(left, first, dims) + dot16(left, second, dims)


def dot_two(left, right, dims):
    first, second = split16(left)
    top, rest = split16(right)
    return dot16(first, top, dims) + (dot16(first, rest, dims) + dot16(second, top, dims))


def eliminate(systems, group=16):
    size, width = systems[0].shape
    rows = lax.broadcasted_iota(jnp.int32, (size, width), 0)
    scales = [jnp.zeros((size, width), F32) for system in systems]
    for start in range(0, size, group):
        for at, system in enumerate(systems):
            columns = [
                jnp.broadcast_to(system[:, k : k + 1], (size, width)) for k in range(start, start + group)
            ]
            for place, k in enumerate(range(start, start + group)):
                inverse = 1.0 / columns[place][k : k + 1, :]
                here = rows == k
                factors = jnp.where(here, 0.0, columns[place])
                scales[at] = jnp.where(here, inverse, scales[at])
                for later in range(place + 1, group):
                    columns[later] = columns[later] - factors * (columns[later][k : k + 1, :] * inverse)
                system = system - factors * (system[k : k + 1, :] * inverse)
            systems[at] = system
    return [(system * scale)[:, size:] for system, scale in zip(systems, scales)]


def compact(block):
    size, width = block.shape
    whole = width - width % 128
    rows = [block[:, at : at + 128] for at in range(0, whole, 128)]
    if whole < width:
        each = size * (width - whole) // 128
        tail = [block[at : at + each, whole:] for at in range(0, size, each)]
        rows.append(jnp.concatenate(tail, 1))
    return jnp.concatenate(rows, 0)


def spread(rows, size):
    width = rows.shape[0] * 128 // size
    whole, rest = width // 128, width % 128
    columns = [rows[k * size : (k + 1) * size] for k in range(whole)]
    if rest:
        tail = rows[whole * size :]
        columns.append(jnp.concatenate([tail[:, at : at + rest] for at in range(0, 128, rest)], 0))
    return jnp.concatenate(columns, 1)


def pack(block, grams):
    size = grams.shape[0]
    rows = lax.broadcasted_iota(jnp.int32, (size, size), 0)
    columns = lax.broadcasted_iota(jnp.int32, (size, size), 1)
    both = jnp.where(rows >= columns, grams[:, :size], grams[:, size:])
    diagonal = jnp.sum(jnp.where(rows == columns, grams[:, size:], 0.0), axis=0, keepdims=True)
    parts = jnp.concatenate(split16(both), 1)
    last = jnp.concatenate(split16(jnp.broadcast_to(diagonal, (16, size))), 1)
    return jnp.concatenate([compact(block), parts, last], 0)


def unpack(messages, size):
    end = messages[0].shape[0]
    blocks, parts, last = (
        sum(message[rows].astype(F32) for message in messages)
        for rows in (slice(0, end - 16 - size), slice(end - 16 - size, end - 16), slice(end - 16, end))
    )
    both = parts[:, :size] + parts[:, size:]
    diagonal = (last[:, :size] + last[:, size:])[:1]
    rows = lax.broadcasted_iota(jnp.int32, (size, size), 0)
    columns = lax.broadcasted_iota(jnp.int32, (size, size), 1)
    turned = both.T
    first = jnp.where(rows >= columns, both, turned)
    second = jnp.where(rows < columns, both, turned)
    second = jnp.where(rows == columns, diagonal, second)
    return spread(blocks, size), jnp.concatenate([first, second], 1)


def held_slots(count, slots, work):
    group = 4 if slots % 4 == 0 else 1

    def turn(g, carry):
        for u in range(group):
            work(g * group + u, g * group + u < count)
        return carry

    lax.fori_loop(0, (count + group - 1) // group, turn, 0)


def places(rows_list, cols_list, n_chip):
    row, column = lax.axis_index("row"), lax.axis_index("col")

    def place(slot):
        apart = rows_list[slot] ^ column
        return (apart % 2) * n_chip + apart // 2, cols_list[slot] ^ row

    return place


def round_kernel(value, out):
    out[...] = compact(value[...].astype(BF16))


def turn_kernel(counts, tiles, after, out):
    def work(slot, held):
        out[slot] = tiles[slot].T

    held_slots(counts[0], tiles.shape[0], work)


def forward_kernel(counts, rows_list, cols_list, tiles, *rest, n_row, dims):
    far_in = rest[:n_row]
    give_core, acc, far = rest[n_row:]
    n_chip = give_core.shape[0]
    slots = tiles.shape[0]
    place = places(rows_list, cols_list, n_chip)
    for d, block in enumerate(far_in):
        far[d] = spread(block[...], far.shape[1])
    acc[...] = jnp.zeros_like(acc)

    def work(slot, held):
        i, j = place(slot)
        acc[i] += jnp.where(held, dot16(far[j], tiles[slot], dims), 0.0)

    held_slots(counts[0], slots, work)
    for d in range(n_chip):
        give_core[d] = acc[n_chip + d].astype(BF16)


def own_kernel(near, diag, residual, after, own_out, grams):
    size = residual.shape[0]
    block = spread(near[...], size)
    own = dot16(block, diag[...], NT)
    own_out[...] = own
    half = 0.5 * dot_exact16(block, own, NT)
    grams[:, :size] = half + half.T
    grams[:, size:] = dot_two(residual[...], residual[...], NT)


def gram_kernel(acc, came, grams_own, *rest):
    *near, keep, grams = rest
    size = grams.shape[0]
    half = jnp.zeros((size, size), F32)
    for d, block in enumerate(near):
        both = acc[d] + came[d].astype(F32)
        keep[d] = both
        half += dot_exact16(spread(block[...], size), both, NT)
    grams[:, :size] = grams_own[:, :size] + half + half.T
    grams[:, size:] = grams_own[:, size:]


def mirrored_kernel(counts, rows_list, cols_list, near_own, near_far, tiles, acc, near):
    n_chip = near_own.shape[0]
    slots = tiles.shape[0]
    place = places(rows_list, cols_list, n_chip)
    for d in range(n_chip):
        near[d] = spread(near_own[d], near.shape[1])
        near[n_chip + d] = spread(near_far[d], near.shape[1])
    acc[...] = jnp.zeros_like(acc)

    def work(slot, held):
        i, j = place(slot)
        acc[j] += jnp.where(held, dot16(near[i], tiles[slot], NN), 0.0)

    held_slots(counts[0], slots, work)


def join_kernel(keep, grams, grams_came, grams_out, *give):
    total = grams[...] + grams_came[...]
    grams_out[...] = total
    for d in range(1, keep.shape[0]):
        give[d - 1][...] = pack(keep[d].astype(BF16), total)


def rows_kernel(keep, grams, own, acc, *rest, n_in):
    image, total, (mine_out, grams_out, *give) = gather_sums(keep[0], grams[...], rest, n_in)
    mine_out[...] = image + own[...] + acc[0]
    grams_out[...] = total
    for d in range(1, acc.shape[0]):
        give[d - 1][...] = pack(acc[d].astype(BF16), total)


def gather_sums(mine, grams, rest, n_in):
    block, matrices = unpack([message[...] for message in rest[:n_in]], mine.shape[0])
    return mine + block, grams + matrices, rest[n_in:]


def first_kernel(mine, grams, probes, *rest, n_in):
    image, total, (image_out, residual_out, rounded, totals, alpha_out) = gather_sums(
        mine[...], grams[...], rest, n_in
    )
    (alpha,) = eliminate([total])
    residual = probes[...] - dot_two(alpha, image, TN)
    rounded[...] = compact(residual.astype(BF16))
    residual_out[...] = residual
    image_out[...] = image
    totals[...] = total
    alpha_out[...] = alpha


def between_kernel(totals, alpha, probes, inverse_out, middle_out, solved_out):
    size = alpha.shape[0]
    eye = (
        lax.broadcasted_iota(jnp.int32, (size, size), 0)
        == lax.broadcasted_iota(jnp.int32, (size, size), 1)
    ).astype(F32)
    (inverse,) = eliminate([jnp.concatenate([totals[:, size:], eye], 1)])
    inverse_out[...] = inverse
    middle_out[...] = dot32(inverse, dot32(totals[:, :size], inverse, NN), TN)
    solved_out[...] = dot_two(alpha[...], probes[...], TN)


def last_kernel(mine, grams, probes, image_in, residual_in, inverse, middle, solved, *rest, n_in):
    forward, total, (solution_out, residual_out) = gather_sums(mine[...], grams[...], rest, n_in)
    size = forward.shape[0]
    norm = total[:, size:]
    curv = total[:, :size] - dot32(norm, dot32(middle[...], norm, NN), TN)
    beta = dot32(inverse[...], norm, NN)
    residual = residual_in[...]
    direction = residual + dot_two(beta, probes[...], TN)
    image = forward + dot_two(beta, image_in[...], TN)
    (step,) = eliminate([jnp.concatenate([curv, norm], 1)])
    solution_out[...] = solved[...] + dot_two(step, direction, TN)
    residual_out[...] = residual - dot_two(step, image, TN)


def call(kernel, outs, args, specs=None, scratch=(), limit=24, name=None, work=None):
    return pl.pallas_call(
        kernel,
        out_shape=outs,
        in_specs=[VMEM] * len(args) if specs is None else specs,
        out_specs=[VMEM] * len(outs),
        scratch_shapes=list(scratch),
        compiler_params=pltpu.CompilerParams(vmem_limit_bytes=limit << 20),
        cost_estimate=None if work is None else pl.CostEstimate(flops=work, bytes_accessed=0, transcendentals=0),
        name=name,
    )(*args)


def body(n_row, n_col, tiles, diag_tiles, probes, rows_list, cols_list, counts):
    n_chip = n_col // 2
    p_size, width = probes.shape[1:]
    shape = jax.ShapeDtypeStruct
    block32 = shape((p_size, width), F32)
    block16 = shape((p_size * width // 128, 128), BF16)

    def over(value, axis, delta):
        size = n_row if axis == "row" else n_col
        return lax.ppermute(value, axis, [(i, i ^ delta) for i in range(size)])

    def over_chips(value):
        return [over(value, "col", 2 * d) for d in range(1, n_chip)]

    def to_rows(values):
        far = [over(value, "row", d) for d, value in enumerate(values[1:], 2)]
        return [over(values[0], "row", 1), *far]

    def over_rows(value):
        return to_rows([value] * (n_row - 1))

    index = [counts[0], rows_list[0, 0], cols_list[0, 0]]
    probes = probes[0]
    diag = diag_tiles[0]
    held = tiles[0, 0]
    square = shape((p_size, 2 * p_size), F32)
    slots = tiles.shape[2]
    passes = 2 * slots * p_size * width * width

    message = shape((block16.shape[0] + p_size + 16, 128), BF16)

    def apply_operator(rounded, residual, turned=None):
        from_rows = over_rows(rounded)
        near = over_chips(rounded)
        give_core, acc_row = call(
            functools.partial(forward_kernel, n_row=n_row, dims=NT if turned is None else NN),
            [shape((n_chip, p_size, width), BF16), shape((n_col, p_size, width), F32)],
            [*index, held if turned is None else turned, rounded, *from_rows],
            [SMEM] * 3 + [VMEM] * (1 + n_row),
            [pltpu.VMEM((n_row, p_size, width), BF16)],
            name="forward",
            work=1,
        )
        give_core, *near = lax.optimization_barrier((give_core, *near))
        came = over(give_core, "col", 1)
        own, grams = call(
            own_kernel, [block32, square], [rounded, diag, residual, acc_row], [VMEM] * 3 + [ANY], name="own"
        )
        near_own = jnp.stack([rounded, *near])
        near_far = over(near_own, "col", 1)
        keep, grams = call(
            gram_kernel,
            [shape((n_chip, p_size, width), F32), square],
            [acc_row, came, grams, rounded, *near],
            name="gram",
        )
        grams_came = over(grams, "col", 1)
        grams, *give = call(
            join_kernel, [square] + [message] * (n_chip - 1), [keep, grams, grams_came], name="join"
        )
        parts = [over(block, "col", 2 * d + 2) for d, block in enumerate(give)]
        (acc_col,) = call(
            mirrored_kernel,
            [shape((n_row, p_size, width), F32)],
            [*index, near_own, near_far, held],
            [SMEM] * 3 + [VMEM] * 3,
            [pltpu.VMEM((n_col, p_size, width), BF16)],
            name="mirrored",
            work=passes,
        )
        mine, grams, *give = call(
            functools.partial(rows_kernel, n_in=n_chip - 1),
            [block32, square] + [message] * (n_row - 1),
            [keep, grams, own, acc_col, *parts],
            name="rows",
        )
        parts = to_rows(give)
        if turned is None:
            (turned,) = call(
                turn_kernel,
                [shape(held.shape, BF16)],
                [index[0], held, grams],
                [SMEM, VMEM, ANY],
                name="turn",
                limit=28,
            )
            turned, *parts = lax.optimization_barrier((turned, *parts))
        return mine, grams, parts, turned

    small = shape((p_size, p_size), F32)
    (rounded,) = call(round_kernel, [block16], [probes], name="round", work=START)
    mine, grams, parts, turned = apply_operator(rounded, probes)
    image, residual, rounded, totals, alpha = call(
        functools.partial(first_kernel, n_in=n_row - 1),
        [block32, block32, block16, square, small],
        [mine, grams, probes, *parts],
        name="first_step",
    )
    inverse, middle, solved = call(
        between_kernel, [small, small, block32], [totals, alpha, probes], name="between"
    )
    mine, grams, parts, turned = apply_operator(rounded, residual, turned)
    solved, residual = call(
        functools.partial(last_kernel, n_in=n_row - 1),
        [block32, block32],
        [mine, grams, probes, image, residual, inverse, middle, solved, *parts],
        name="last_step",
    )
    return solved[None], residual[None]


def solution(mesh):
    placed = (
        P("row", "col", None, None, None),
        P(("row", "col"), None, None),
        P(("row", "col"), None, None),
        P("row", "col", None),
        P("row", "col", None),
        P("row", "col"),
    )
    return jax.shard_map(
        functools.partial(body, mesh.shape["row"], mesh.shape["col"]),
        mesh=mesh,
        in_specs=placed,
        out_specs=(P(("row", "col"), None, None), P(("row", "col"), None, None)),
        check_vma=False,
    )
```
